32 devices in a mesh: wide: 16 (over z, y, x), narrow: 2 (over core).
Axes of the slice: x: 2, y: 2, z: 4, core: 2. Of those that a mesh axis runs over, the one named last changes fastest.
Arguments:
- points: bfloat16 [32, 1024, 512], P('wide', 'narrow'), may hold values from -6 to 6
- counts: int32 [32, 256], P('wide', 'narrow'), may hold values from 1 to 4, as said below
- destination: int32 [32, 256], P('wide', 'narrow'), may hold values from 0 to 15, as said below
- rotated_ball: int32 [32, 256], P('wide', 'narrow'), may hold values from 0 to 1
- qkv_first: bfloat16 [512, 1536], replicated, may hold values from -1 to 1
- out_first: bfloat16 [512, 512], replicated, may hold values from -0.25 to 0.25
- qkv_second: bfloat16 [512, 1536], replicated, may hold values from -1 to 1
- out_second: bfloat16 [512, 512], replicated, may hold values from -0.25 to 0.25
Outputs:
- result: bfloat16 [32, 1024, 512], P('wide', 'narrow')
The draws below stay inside these ranges and needn't reach their ends.
Inputs may be any that keep to these rules, and one draw needn't show every extreme that they name: `counts`: the first block of every ball row has all 4 points usable. Among the blocks of one device, at most 32 have the same destination; on every device some destination receives 32 of its blocks, and some destination receives 32 blocks from every device of its narrow index.
All inputs are finite; a program needn't handle non-finite values.
Results may differ from the reference program's by a relative error of at most 0.0095.
Values may be sent and summed in bfloat16 or wider, within the bound.
No kernel may reach another device: no remote copies, remote signals or barrier semaphores. Data moves between devices by JAX's collectives and lax.ppermute only.
A program may use at most 128 MiB of HBM per device.

```python
import math
import jax
import jax.numpy as jnp
from jax import lax

D = 512
HEADS = 8
BALL = 1024
BLK = 4
ROT_BALLS = 2
BALLS_DEV = 2
BALLS = 32
CAP = 32
N_WIDE = 16
N_NARROW = 2


def drawn_weight(key, marker):
    noise = jax.random.normal(jax.random.fold_in(key, marker), (D, 3 * D), jnp.float32)
    weight = jnp.clip(noise, -4.0, 4.0) * (1.0 / math.sqrt(D))
    return weight.astype(jnp.bfloat16)


def draw_points(key, part):
    noise = jax.random.normal(jax.random.fold_in(key, 11), (BALLS, BALL, D), jnp.float32)
    values = jnp.clip(noise, -6.0, 6.0)
    return values.astype(jnp.bfloat16)


def draw_qkv_first(key, part):
    return drawn_weight(key, 21)


def draw_qkv_second(key, part):
    return drawn_weight(key, 31)


def draw_counts(key, part):
    raw_counts = jax.random.randint(key, (BALLS, BALL // BLK), 1, BLK + 1, dtype=jnp.int32)
    return raw_counts.at[:, 0].set(BLK)


def draw_destination(key, part):
    sub_blocks = BALL // N_NARROW // BLK
    block_count = BALLS_DEV * sub_blocks
    slot_total = N_WIDE * CAP
    hotness = jax.random.randint(jax.random.fold_in(key, 1), (N_WIDE,), 0, 8, dtype=jnp.int32)
    hottest = jax.random.randint(jax.random.fold_in(key, 2), (), 0, N_WIDE, dtype=jnp.int32)
    hotness = hotness.at[hottest].set(8)
    hotness = hotness.at[0].set(8)
    hotness = hotness.at[N_WIDE - 1].set(8)
    slot_dest = jnp.arange(slot_total, dtype=jnp.int32) // CAP

    def one_device(device_key):
        noise = jax.random.randint(device_key, (slot_total,), 0, 256, dtype=jnp.int32)
        scores = (hotness[slot_dest] * 256 + noise) * slot_total + jnp.arange(slot_total, dtype=jnp.int32)
        chosen = lax.top_k(scores, block_count)[1]
        picked = slot_dest[chosen]
        order = jax.random.permutation(jax.random.fold_in(device_key, 7), block_count)
        return picked[order]
    device_keys = jax.random.split(jax.random.fold_in(key, 3), N_WIDE * N_NARROW)
    lists = jax.vmap(one_device)(device_keys)
    shaped = lists.reshape(N_WIDE, N_NARROW, BALLS_DEV, sub_blocks)
    return jnp.transpose(shaped, (0, 2, 1, 3)).reshape(BALLS, BALL // BLK).astype(jnp.int32)


def touch_ends(values, key, smallest, high):
    shape = values.shape
    index_at = [jax.random.randint(jax.random.fold_in(key, axis), (), 0, shape[axis]) for axis in range(len(shape))]
    values = values.at[tuple(index_at)].set(smallest)
    longest = shape.index(max(shape))
    index_at[longest] = (index_at[longest] + 1) % shape[longest]
    return values.at[tuple(index_at)].set(high)


def scatter_about(key, extent, spread, reach, kind=jnp.bfloat16):
    values = jax.random.normal(key, extent, jnp.float32) * spread
    return jnp.minimum(jnp.maximum(values, -reach), reach).astype(kind)


def setup_inputs(seed: int = 0) -> dict:
    arg_keys = jax.random.split(jax.random.key(seed), 9)
    return {
        "points": draw_points(jax.random.fold_in(arg_keys[8], 71), 0),
        "counts": draw_counts(jax.random.fold_in(arg_keys[8], 71), 0),
        "destination": draw_destination(jax.random.fold_in(arg_keys[8], 71), 0),
        "rotated_ball": touch_ends(jax.random.randint(arg_keys[3], (BALLS, BALL // BLK), 0, ROT_BALLS), jax.random.fold_in(arg_keys[3], 1), 0, ROT_BALLS - 1).astype(jnp.int32),
        "qkv_first": draw_qkv_first(jax.random.fold_in(arg_keys[8], 71), 0),
        "out_first": scatter_about(arg_keys[5], (D, D), D ** -0.5, 0.25),
        "qkv_second": draw_qkv_second(jax.random.fold_in(arg_keys[8], 71), 0),
        "out_second": scatter_about(arg_keys[7], (D, D), D ** -0.5, 0.25),
    }


EPSILON = 1e-06
NEGATIVE = -1e+30

def rms_round(values):
    widened = values.astype(jnp.float32)
    scaled = widened * lax.rsqrt(lax.optimization_barrier(jnp.mean(widened * widened, axis=-1, keepdims=True)) + EPSILON)
    return scaled.astype(jnp.bfloat16)

def project(normed, weight):
    flat = normed.reshape(-1, normed.shape[-1])
    product = jnp.dot(flat, weight, preferred_element_type=jnp.float32)
    return product.reshape(normed.shape[:-1] + (weight.shape[1],))

def split_heads(block_rows, offset, model_width):
    head_dim = model_width // HEADS
    return block_rows[..., offset:offset + model_width].reshape(block_rows.shape[:-1] + (HEADS, head_dim)).astype(jnp.float32)

def usable_points(counts):
    position = lax.broadcasted_iota(jnp.int32, counts.shape + (BLK,), len(counts.shape))
    usable = position < counts[..., None]
    return usable.reshape(counts.shape[:-1] + (counts.shape[-1] * BLK,))

def pool_rows(qkv_all, counts):
    model_width = qkv_all.shape[-1] // 3
    usable = usable_points(counts)
    kv_part = qkv_all[..., model_width:].astype(jnp.float32) * usable[..., None].astype(jnp.float32)
    grouped = kv_part.reshape(counts.shape + (BLK, 2 * model_width)).sum(axis=-2)
    return (grouped / counts[..., None].astype(jnp.float32)).astype(jnp.bfloat16)

def fine_coarse(ball_qkv, fine_usable, coarse_kv):
    model_width = coarse_kv.shape[-1] // 2
    scaling = 1.0 / math.sqrt(model_width // HEADS)
    queries = split_heads(ball_qkv, 0, model_width)
    key_fine = split_heads(ball_qkv, model_width, model_width)
    value_fine = split_heads(ball_qkv, 2 * model_width, model_width)
    key_coarse = split_heads(coarse_kv, 0, model_width)
    value_coarse = split_heads(coarse_kv, model_width, model_width)
    score_fine = jnp.einsum('qhe,khe->hqk', queries, key_fine) * scaling
    score_fine = jnp.where(fine_usable[None, None, :], score_fine, NEGATIVE)
    score_coarse = jnp.einsum('qhe,khe->hqk', queries, key_coarse) * scaling
    highest = jnp.maximum(lax.optimization_barrier(jnp.max(score_fine, axis=-1)), lax.optimization_barrier(jnp.max(score_coarse, axis=-1)))[..., None]
    exp_fine = jnp.exp(score_fine - highest)
    exp_coarse = jnp.exp(score_coarse - highest)
    denominator = lax.optimization_barrier(jnp.sum(exp_fine, axis=-1, keepdims=True)) + lax.optimization_barrier(jnp.sum(exp_coarse, axis=-1, keepdims=True))
    weight_fine = (exp_fine / denominator).astype(jnp.bfloat16).astype(jnp.float32)
    weight_coarse = (exp_coarse / denominator).astype(jnp.bfloat16).astype(jnp.float32)
    mixture = jnp.einsum('hqk,khe->qhe', weight_fine, value_fine) + jnp.einsum('hqk,khe->qhe', weight_coarse, value_coarse)
    return mixture.reshape(mixture.shape[0], model_width).astype(jnp.bfloat16)

def ball_attention(recv_rows, row_ball, row_usable):
    total_rows = recv_rows.shape[0]
    model_width = recv_rows.shape[1] // 3
    scaling = 1.0 / math.sqrt(model_width // HEADS)
    queries = split_heads(recv_rows, 0, model_width)
    key_rows = split_heads(recv_rows, model_width, model_width)
    value_rows = split_heads(recv_rows, 2 * model_width, model_width)
    block_len = min(256, total_rows)

    def one_block(block_idx):
        offset = (block_idx * block_len).astype(jnp.int32)
        query_block = lax.dynamic_slice_in_dim(queries, offset, block_len, 0)
        ball_block = lax.dynamic_slice_in_dim(row_ball, offset, block_len, 0)
        scores = jnp.einsum('qhe,khe->hqk', query_block, key_rows) * scaling
        allowed = (ball_block[:, None] == row_ball[None, :]) & row_usable[None, :]
        scores = jnp.where(allowed[None], scores, NEGATIVE)
        highest = lax.optimization_barrier(jnp.max(scores, axis=-1, keepdims=True))
        exponent = jnp.exp(scores - highest)
        weights = (exponent / lax.optimization_barrier(jnp.sum(exponent, axis=-1, keepdims=True))).astype(jnp.bfloat16).astype(jnp.float32)
        mixture = jnp.einsum('hqk,khe->qhe', weights, value_rows)
        return mixture.reshape(block_len, model_width).astype(jnp.bfloat16)
    blocks_out = lax.map(one_block, jnp.arange(total_rows // block_len, dtype=jnp.int32))
    return blocks_out.reshape(total_rows, model_width)

def by_source(array_in, sub_blocks):
    rest = array_in.shape[2:]
    shaped = array_in.reshape((N_WIDE, BALLS_DEV, N_NARROW, sub_blocks) + rest)
    moved = jnp.moveaxis(shaped, 2, 0)
    return moved.reshape((N_NARROW, N_WIDE, BALLS_DEV * sub_blocks) + rest)

def from_source(array_in, sub_blocks):
    rest = array_in.shape[3:]
    shaped = array_in.reshape((N_NARROW, N_WIDE, BALLS_DEV, sub_blocks) + rest)
    moved = jnp.moveaxis(shaped, 0, 2)
    return moved.reshape((BALLS, N_NARROW * sub_blocks) + rest)

def reference(points, counts, destination, rotated_ball, qkv_first, out_first, qkv_second, out_second):
    model_width = points.shape[-1]
    share = BALL // N_NARROW
    sub_blocks = share // BLK
    normed_one = rms_round(points)
    qkv_one = project(normed_one, qkv_first).astype(jnp.bfloat16)
    pooled = pool_rows(qkv_one, counts)
    usable = usable_points(counts)

    def per_ball(ball_idx):
        ball_qkv = qkv_one[ball_idx].reshape(N_NARROW, share, 3 * model_width)
        ball_usable = usable[ball_idx].reshape(N_NARROW, share)
        attended = jax.vmap(fine_coarse, in_axes=(0, 0, None))(ball_qkv, ball_usable, pooled[ball_idx])
        return attended.reshape(BALL, model_width)
    attended_one = lax.map(per_ball, jnp.arange(BALLS, dtype=jnp.int32))
    layer_one = (points.astype(jnp.float32) + project(attended_one, out_first)).astype(jnp.bfloat16)
    normed_two = rms_round(layer_one)
    qkv_two = project(normed_two, qkv_second).astype(jnp.bfloat16)
    qkv_source = by_source(qkv_two.reshape(BALLS, BALL // BLK, BLK, 3 * model_width), sub_blocks)
    dest_source = by_source(destination, sub_blocks)
    ball_source = by_source(rotated_ball, sub_blocks)
    count_source = by_source(counts, sub_blocks)
    onehot = (dest_source[..., None] == jnp.arange(N_WIDE, dtype=jnp.int32)).astype(jnp.int32)
    earlier = jnp.cumsum(onehot, axis=2, dtype=jnp.int32) - onehot
    rank_in = lax.optimization_barrier(jnp.sum(earlier * onehot, axis=-1, dtype=jnp.int32))
    narrow_idx = lax.broadcasted_iota(jnp.int32, dest_source.shape, 0)
    wide_idx = lax.broadcasted_iota(jnp.int32, dest_source.shape, 1)
    block_idx = lax.broadcasted_iota(jnp.int32, dest_source.shape, 2)
    table = jnp.full((N_NARROW, N_WIDE, N_WIDE, CAP), -1, jnp.int32)
    table = table.at[narrow_idx, dest_source, wide_idx, rank_in].set(block_idx)
    sources = jnp.arange(N_WIDE, dtype=jnp.int32)[:, None]

    def receive(pair):
        narrow_at = pair // N_WIDE
        recv_at = pair % N_WIDE
        picks = table[narrow_at, recv_at]
        live = picks >= 0
        safe_pick = jnp.maximum(picks, 0)
        block_rows = qkv_source[narrow_at][sources, safe_pick]
        block_rows = jnp.where(live[..., None, None], block_rows, jnp.zeros_like(block_rows))
        ball_ids = jnp.where(live, ball_source[narrow_at][sources, safe_pick], -1)
        fill_in = jnp.where(live, count_source[narrow_at][sources, safe_pick], 0)
        row_ball = jnp.broadcast_to(ball_ids[..., None], ball_ids.shape + (BLK,)).reshape(-1)
        row_usable = usable_points(fill_in).reshape(-1)
        return ball_attention(block_rows.reshape(-1, 3 * model_width), row_ball, row_usable)
    received = lax.map(receive, jnp.arange(N_NARROW * N_WIDE, dtype=jnp.int32))
    received = received.reshape(N_NARROW, N_WIDE, N_WIDE, CAP, BLK, model_width)
    back_source = received[narrow_idx, dest_source, wide_idx, rank_in]
    attended_two = from_source(back_source, sub_blocks).reshape(BALLS, BALL, model_width)
    return (layer_one.astype(jnp.float32) + project(attended_two, out_second)).astype(jnp.bfloat16)
```

```python
import functools
import math

import jax
import jax.numpy as jnp
from jax import lax
from jax.experimental import pallas as pl
from jax.experimental.pallas import tpu as pltpu
from jax.sharding import PartitionSpec as P

HEADS = 8
BLK = 4
EPSILON = 1e-06
NEGATIVE = -1e30
LANES = 128
TILE = 256
VMEM_LIMIT = 56 * 1024 * 1024
BF16 = jnp.bfloat16
F32 = jnp.float32
I32 = jnp.int32

NT = (((1,), (1,)), ((), ()))


def iota(shape, axis):
    return lax.broadcasted_iota(I32, shape, axis)


def mm(left, right):
    return jnp.dot(left, right, preferred_element_type=F32)


def mm_t(left, right):
    return lax.dot_general(left, right, NT, preferred_element_type=F32)


def params():
    return pltpu.CompilerParams(vmem_limit_bytes=VMEM_LIMIT)


def whole(array):
    return pl.BlockSpec(array.shape, lambda *_: (0,) * len(array.shape))


def normalize(rows):
    return (rows * lax.rsqrt(jnp.mean(rows * rows, axis=-1, keepdims=True) + EPSILON)).astype(BF16)


def project_rows(normed, weight, width):
    factor = math.log2(math.e) / math.sqrt(width // HEADS)
    query = (mm(normed, weight[:, :width]) * factor).astype(BF16)
    return query, mm(normed, weight[:, width:]).astype(BF16)


def head_pair(query, parts, masks):
    lane = iota(query.shape, 1)
    half = LANES // 2
    results = []
    for head in range(2):
        own = (lane < half) if head == 0 else (lane >= half)
        q = jnp.where(own, query, jnp.zeros_like(query))
        scores = [mm_t(q, keys) for keys, _ in parts]
        scores = [s if mask is None else mask(s) for s, mask in zip(scores, masks)]
        highest = functools.reduce(
            jnp.maximum, [jnp.max(s, axis=-1, keepdims=True) for s in scores]
        )
        total = None
        for s, (_, values) in zip(scores, parts):
            p = jnp.exp2(s - highest).astype(BF16)
            wide = jnp.concatenate([values, jnp.ones_like(values)], axis=1)
            part = mm(p, wide)
            total = part if total is None else total + part
        results.append(total[:, :LANES] / total[:, LANES:])
    return jnp.where(lane < half, results[0], results[1])


def first_projection_kernel(width, points_ref, fill_ref, weight_ref, query_ref, kv_ref, pooled_ref):
    normed = normalize(points_ref[0].astype(F32))
    query, kv = project_rows(normed, weight_ref, width)
    query_ref[0] = query
    kv_ref[0] = kv
    share = normed.shape[0]
    blocks = share // BLK
    block = iota((blocks, share), 0)
    point = iota((blocks, share), 1)
    member = (point // BLK == block) & (point % BLK < fill_ref[0])
    chosen = jnp.where(member, 1.0, 0.0)
    count = jnp.sum(chosen, axis=1, keepdims=True)
    pooled_ref[0] = (mm(chosen.astype(BF16), kv) / count).astype(BF16)


def first_projection(points, fill_row, weight):
    balls, share, width = points.shape
    blocks = share // BLK
    ball = lambda rows, cols: pl.BlockSpec((1, rows, cols), lambda b: (b, 0, 0))
    return pl.pallas_call(
        functools.partial(first_projection_kernel, width),
        grid=(balls,),
        in_specs=[ball(share, width), ball(1, share), whole(weight)],
        out_specs=[ball(share, width), ball(share, 2 * width), ball(blocks, 2 * width)],
        out_shape=[
            jax.ShapeDtypeStruct((balls, share, width), BF16),
            jax.ShapeDtypeStruct((balls, share, 2 * width), BF16),
            jax.ShapeDtypeStruct((balls, blocks, 2 * width), BF16),
        ],
        compiler_params=params(),
        cost_estimate=pl.CostEstimate(
            flops=2 * balls * share * width * 3 * width, bytes_accessed=8 * balls * share * width,
            transcendentals=0,
        ),
        name="first_projection",
    )(points, fill_row, weight)


def first_attention_kernel(
    width, query_ref, kv_ref, coarse_ref, fill_ref, points_ref, out_ref, slot_ref,
    layer_ref, packed_ref, attended, normed_all,
):
    ball = pl.program_id(0)
    share = points_ref.shape[1]
    tile = min(TILE, share)
    position = iota((1, share), 1)
    bias = jnp.where(position % BLK < fill_ref[0], 0.0, NEGATIVE)

    def one_pair(pair, carry):
        at = pl.multiple_of(pair * LANES, LANES)
        value_at = pl.multiple_of(width + pair * LANES, LANES)
        keys, values = kv_ref[0, :, pl.ds(at, LANES)], kv_ref[0, :, pl.ds(value_at, LANES)]
        coarse_keys = coarse_ref[0, :, pl.ds(at, LANES)]
        coarse_values = coarse_ref[0, :, pl.ds(value_at, LANES)]
        for row in range(0, share, tile):
            mixture = head_pair(
                query_ref[0, pl.ds(row, tile), pl.ds(at, LANES)],
                [(keys, values), (coarse_keys, coarse_values)],
                [lambda s: s + bias, None],
            )
            attended[pl.ds(row, tile), pl.ds(at, LANES)] = mixture.astype(BF16)
        return carry

    lax.fori_loop(0, width // LANES, one_pair, 0)
    layer = points_ref[0].astype(F32) + mm(attended[...], out_ref[...])
    layer = layer.astype(BF16)
    layer_ref[0] = layer
    normed_all[pl.ds(pl.multiple_of(ball * share, share), share), :] = normalize(layer.astype(F32))

    @pl.when(ball == pl.num_programs(0) - 1)
    def _():
        rows = packed_ref.shape[0]
        step = min(TILE, rows)

        def one_tile(index, carry):
            at = pl.multiple_of(index * step, step)
            target = at + iota((step, slot_ref.shape[1]), 0)
            chosen = jnp.where(target == slot_ref[...], 1.0, 0.0).astype(BF16)
            packed_ref[pl.ds(at, step), :] = mm(chosen, normed_all[...]).astype(BF16)
            return carry

        lax.fori_loop(0, rows // step, one_tile, 0)


def first_attention(query, kv, coarse, fill_row, points, weight, slot_row, packed_rows):
    balls, share, width = points.shape
    coarse_rows = coarse.shape[1]
    ball = lambda rows, cols: pl.BlockSpec((1, rows, cols), lambda b: (b, 0, 0))
    return pl.pallas_call(
        functools.partial(first_attention_kernel, width),
        grid=(balls,),
        in_specs=[
            ball(share, width), ball(share, 2 * width), ball(coarse_rows, 2 * width),
            ball(1, share), ball(share, width), whole(weight), whole(slot_row),
        ],
        out_specs=[
            ball(share, width),
            pl.BlockSpec((packed_rows, width), lambda b: (0, 0)),
        ],
        out_shape=[
            jax.ShapeDtypeStruct((balls, share, width), BF16),
            jax.ShapeDtypeStruct((packed_rows, width), BF16),
        ],
        scratch_shapes=[
            pltpu.VMEM((share, width), BF16), pltpu.VMEM((balls * share, width), BF16),
        ],
        compiler_params=params(),
        cost_estimate=pl.CostEstimate(
            flops=16 * balls * share * (share + coarse_rows) * width,
            bytes_accessed=16 * balls * share * width,
            transcendentals=HEADS * balls * share * (share + coarse_rows),
        ),
        name="first_attention",
    )(query, kv, coarse, fill_row, points, weight, slot_row)


def arrange_kernel(width, place_ref, rows_ref, weight_ref, query_ref, kv_ref):
    tile = query_ref.shape[0]
    target = pl.program_id(0) * tile + iota((tile, place_ref.shape[1]), 0)
    chosen = jnp.where(target == place_ref[...], 1.0, 0.0).astype(BF16)
    normed = mm(chosen, rows_ref[...]).astype(BF16)
    query, kv = project_rows(normed, weight_ref, width)
    query_ref[...] = query
    kv_ref[...] = kv


def arrange(place_row, rows, weight, tile, sorted_rows):
    count, width = rows.shape
    out = lambda cols: pl.BlockSpec((tile, cols), lambda t: (t, 0))
    return pl.pallas_call(
        functools.partial(arrange_kernel, width),
        grid=(sorted_rows // tile,),
        in_specs=[whole(place_row), whole(rows), whole(weight)],
        out_specs=[out(width), out(2 * width)],
        out_shape=[
            jax.ShapeDtypeStruct((sorted_rows, width), BF16),
            jax.ShapeDtypeStruct((sorted_rows, 2 * width), BF16),
        ],
        compiler_params=params(),
        cost_estimate=pl.CostEstimate(
            flops=2 * sorted_rows * width * (count + 3 * width),
            bytes_accessed=8 * sorted_rows * width, transcendentals=0,
        ),
        name="arrange",
    )(place_row, rows, weight)


def rotated_attention_kernel(
    tile, limits_ref, place_ref, query_ref, key_ref, value_ref, mixture_ref, attended
):
    pairs = query_ref.shape[1] // LANES
    sorted_rows = query_ref.shape[0]

    def attend(start, usable, tiles, first_query, pair):
        at = pl.multiple_of(pair * LANES, LANES)
        lanes = pl.ds(at, LANES)
        whole_keys = (tiles - 1) * tile
        edge = usable - whole_keys
        parts, masks = [], []
        if whole_keys:
            span = pl.ds(pl.multiple_of(start, tile), whole_keys)
            parts.append((key_ref[span, lanes], value_ref[span, lanes]))
            masks.append(None)
        span = pl.ds(pl.multiple_of(start + whole_keys, tile), tile)
        parts.append((key_ref[span, lanes], value_ref[span, lanes]))
        masks.append(lambda s: jnp.where(iota(s.shape, 1) < edge, s, NEGATIVE))
        rows = pl.ds(pl.multiple_of(first_query, tile), tile)
        mixture = head_pair(query_ref[rows, lanes], parts, masks)
        attended[rows, lanes] = mixture.astype(BF16)

    attended[...] = jnp.zeros_like(attended)
    for ball in range(limits_ref.shape[0]):
        start, rows, usable = (limits_ref[ball, i] for i in range(3))
        key_tiles = (usable + tile - 1) // tile
        query_tiles = (rows + tile - 1) // tile
        for tiles in range(1, sorted_rows // tile):

            @pl.when(key_tiles == tiles)
            def _(tiles=tiles):
                def one(step, carry):
                    attend(start, usable, tiles, start + (step // pairs) * tile, step % pairs)
                    return carry

                lax.fori_loop(0, query_tiles * pairs, one, 0)

    rows = mixture_ref.shape[0]

    def one_tile(index, carry):
        at = pl.multiple_of(index * tile, tile)
        place = place_ref[pl.ds(at, tile), :]
        chosen = jnp.where(iota((tile, sorted_rows), 1) == place, 1.0, 0.0).astype(BF16)
        mixture_ref[pl.ds(at, tile), :] = mm(chosen, attended[...]).astype(BF16)
        return carry

    lax.fori_loop(0, rows // tile, one_tile, 0)


def rotated_attention(limits, place_column, query, kv, tile, group, groups):
    sorted_rows, width = query.shape
    columns = width // groups
    rows = place_column.shape[0]
    part = lambda offset: pl.BlockSpec((sorted_rows, columns), lambda _: (0, offset + group))
    return pl.pallas_call(
        functools.partial(rotated_attention_kernel, tile),
        grid=(1,),
        in_specs=[
            pl.BlockSpec(memory_space=pltpu.SMEM),
            whole(place_column), part(0), part(0), part(groups),
        ],
        out_specs=pl.BlockSpec((rows, columns), lambda _: (0, 0)),
        out_shape=jax.ShapeDtypeStruct((rows, columns), BF16),
        scratch_shapes=[pltpu.VMEM((sorted_rows, columns), BF16)],
        compiler_params=params(),
        cost_estimate=pl.CostEstimate(
            flops=8 * rows * rows * columns, bytes_accessed=10 * rows * columns,
            transcendentals=rows * rows * HEADS // (2 * groups),
        ),
        name="rotated_attention",
    )(limits, place_column, query, kv, kv)


def finish_kernel(groups, slot_ref, layer_ref, weight_ref, *refs):
    returned, result_ref = refs[:groups], refs[groups]
    share = layer_ref.shape[1]
    columns = returned[0].shape[1]
    target = iota((share, returned[0].shape[0]), 1)
    chosen = jnp.where(target == slot_ref[0], 1.0, 0.0).astype(BF16)
    total = layer_ref[0].astype(F32)
    for group, part in enumerate(returned):
        attended = mm(chosen, part[...]).astype(BF16)
        total = total + mm(attended, weight_ref[pl.ds(group * columns, columns), :])
    result_ref[0] = total.astype(BF16)


def finish(slot_column, layer, weight, returned):
    balls, share, width = layer.shape
    ball = lambda rows, cols: pl.BlockSpec((1, rows, cols), lambda b: (b, 0, 0))
    rows = returned[0].shape[0]
    return pl.pallas_call(
        functools.partial(finish_kernel, len(returned)),
        grid=(balls,),
        in_specs=[ball(share, 1), ball(share, width), whole(weight)]
        + [whole(part) for part in returned],
        out_specs=ball(share, width),
        out_shape=jax.ShapeDtypeStruct(layer.shape, BF16),
        compiler_params=params(),
        cost_estimate=pl.CostEstimate(
            flops=2 * balls * share * width * (rows + width),
            bytes_accessed=8 * balls * share * width, transcendentals=0,
        ),
        name="finish",
    )(slot_column, layer, weight, *returned)


def gather_shares(array, axis_name, axis):
    count = lax.axis_size(axis_name)
    if count & (count - 1):
        return lax.all_gather(array, axis_name, axis=axis, tiled=True)
    index = lax.axis_index(axis_name)
    step = 1
    while step < count:
        other = lax.ppermute(array, axis_name, [(i, i ^ step) for i in range(count)])
        lower = (index & step) == 0
        array = jnp.where(
            lower,
            jnp.concatenate([array, other], axis=axis),
            jnp.concatenate([other, array], axis=axis),
        )
        step *= 2
    return array


def exchange(rows, wide_count):
    parts = rows.reshape((wide_count, rows.shape[0] // wide_count) + rows.shape[1:])
    parts = lax.all_to_all(parts, "wide", split_axis=0, concat_axis=0, tiled=True)
    return parts.reshape(rows.shape)


def earlier_sum(values):
    return jnp.cumsum(values, axis=-1, dtype=I32) - values


def on_device(
    points, counts, destination, rotated_ball, qkv_first, out_first, qkv_second, out_second
):
    balls, share, width = points.shape
    wide_count = lax.axis_size("wide")
    block_count = destination.size
    capacity = max(2, 2 * block_count // wide_count)
    slots = wide_count * capacity
    rows = slots * BLK
    tile = min(TILE, rows)
    groups = 2

    dest_flat = destination.reshape(block_count)
    code = (dest_flat * 2 + rotated_ball.reshape(block_count)) * BLK + counts.reshape(block_count) - 1
    onehot = (
        jnp.arange(wide_count, dtype=I32)[:, None] == dest_flat[None, :]
    ).astype(I32)
    slot_of = dest_flat * capacity + jnp.sum(earlier_sum(onehot) * onehot, axis=0, dtype=I32)
    slot_row = jnp.repeat(slot_of * BLK, BLK) + jnp.tile(jnp.arange(BLK, dtype=I32), block_count)
    fill_row = jnp.repeat(counts, BLK, axis=1).reshape(balls, 1, share)

    query, kv, pooled = first_projection(points, fill_row, qkv_first)
    coarse = gather_shares(pooled, "narrow", 1)
    codes = gather_shares(code.reshape(1, block_count), "wide", 0)
    layer_one, packed = first_attention(
        query, kv, coarse, fill_row, points, out_first, slot_row.reshape(1, -1), rows
    )
    arrived = exchange(packed, wide_count)

    mine = (codes // (2 * BLK)) == lax.axis_index("wide")
    rank = earlier_sum(mine.astype(I32))
    label = jnp.where(mine, codes % (2 * BLK) + 1, 0)
    at_slot = rank[:, None, :] == jnp.arange(capacity, dtype=I32)[None, :, None]
    label = jnp.sum(jnp.where(at_slot, label[:, None, :], 0), axis=-1, dtype=I32).reshape(slots)
    live = label > 0
    ball = jnp.where(live, (label - 1) // BLK, -1)
    fill = jnp.where(live, (label - 1) % BLK + 1, 0)
    member = (ball[None, :] == jnp.arange(2, dtype=I32)[:, None]).astype(I32)
    usable = member * fill[None, :]
    spare = member * (BLK - fill)[None, :]
    usable_total = jnp.sum(usable, axis=1, dtype=I32)
    row_total = jnp.sum(member, axis=1, dtype=I32) * BLK
    second = (row_total[0] + tile - 1) // tile * tile
    starts = jnp.stack([jnp.zeros_like(second), second])
    limits = jnp.stack([starts, row_total, usable_total], axis=1)
    usable_at = jnp.sum(member * (starts[:, None] + earlier_sum(usable)), axis=0, dtype=I32)
    spare_at = jnp.sum(
        member * ((starts + usable_total)[:, None] + earlier_sum(spare)), axis=0, dtype=I32
    )
    point = jnp.arange(BLK, dtype=I32)[None, :]
    place = jnp.where(
        point < fill[:, None], usable_at[:, None] + point, (spare_at - fill)[:, None] + point
    )
    place = jnp.where(live[:, None], place, -1).reshape(rows)

    sorted_rows = rows + tile
    query_two, kv_two = arrange(place.reshape(1, rows), arrived, qkv_second, tile, sorted_rows)
    returned = []
    for group in range(groups):
        mixture = rotated_attention(
            limits, place.reshape(rows, 1), query_two, kv_two, tile, group, groups
        )
        returned.append(exchange(mixture, wide_count))
    return finish(slot_row.reshape(balls, share, 1), layer_one, out_second, returned)


def solution(mesh):
    split = P("wide", "narrow")
    in_specs = (P("wide", "narrow", None), split, split, split, P(), P(), P(), P())
    out_specs = P("wide", "narrow", None)
    return jax.shard_map(
        on_device, mesh=mesh, in_specs=in_specs, out_specs=out_specs, check_vma=False
    )
```

```python
import functools
import math

import jax
import jax.numpy as jnp
from jax import lax
from jax.experimental import pallas as pl
from jax.experimental.pallas import tpu as pltpu
from jax.sharding import PartitionSpec as P

HEADS = 8
BLK = 4
EPSILON = 1e-06
NEGATIVE = -1e30
LANES = 128
TILE = 256
VMEM_LIMIT = 56 * 1024 * 1024
BF16 = jnp.bfloat16
F32 = jnp.float32
I32 = jnp.int32

NT = (((1,), (1,)), ((), ()))


def iota(shape, axis):
    return lax.broadcasted_iota(I32, shape, axis)


def mm(left, right):
    return jnp.dot(left, right, preferred_element_type=F32)


def mm_t(left, right):
    return lax.dot_general(left, right, NT, preferred_element_type=F32)


def params():
    return pltpu.CompilerParams(vmem_limit_bytes=VMEM_LIMIT)


def whole(array):
    return pl.BlockSpec(array.shape, lambda *_: (0,) * len(array.shape))


def normalize(rows):
    return (rows * lax.rsqrt(jnp.mean(rows * rows, axis=-1, keepdims=True) + EPSILON)).astype(BF16)


def project_rows(normed, weight, width):
    factor = math.log2(math.e) / math.sqrt(width // HEADS)
    query = (mm(normed, weight[:, :width]) * factor).astype(BF16)
    return query, mm(normed, weight[:, width:]).astype(BF16)


def block_digits(values):
    digits = jnp.concatenate([values // 32, values % 32] + [jnp.zeros_like(values)] * 6, axis=0)
    return digits.astype(F32).astype(BF16)


def point_row(values):
    blocks = values.shape[1]
    spread = iota((blocks, blocks * BLK), 1) // BLK == iota((blocks, blocks * BLK), 0)
    digits = mm(block_digits(values), jnp.where(spread, 1.0, 0.0).astype(BF16)).astype(I32)
    return (digits[:1] * 32 + digits[1:2]) * BLK + iota((1, blocks * BLK), 1) % BLK


def point_column(values):
    blocks = values.shape[1]
    spread = iota((blocks * BLK, blocks), 0) // BLK == iota((blocks * BLK, blocks), 1)
    digits = mm_t(jnp.where(spread, 1.0, 0.0).astype(BF16), block_digits(values)).astype(I32)
    return (digits[:, :1] * 32 + digits[:, 1:2]) * BLK + iota((blocks * BLK, 1), 0) % BLK


def own_half(lane, head):
    return (lane < LANES // 2) if head == 0 else (lane >= LANES // 2)


def softmax_mix(scores, values):
    highest = functools.reduce(jnp.maximum, [jnp.max(s, axis=-1, keepdims=True) for s in scores])
    total = None
    for s, v in zip(scores, values):
        wide = jnp.concatenate([v, jnp.ones_like(v)], axis=1)
        part = mm(jnp.exp2(s - highest).astype(BF16), wide)
        total = part if total is None else total + part
    return total[:, :LANES] / total[:, LANES:]


def first_projection_kernel(
    width, points_ref, counts_ref, weight_ref, query_ref, kv_ref, pooled_ref, bias_ref
):
    normed = normalize(points_ref[0].astype(F32))
    query, kv = project_rows(normed, weight_ref, width)
    query_ref[0] = query
    kv_ref[0] = kv
    share = normed.shape[0]
    blocks = share // BLK
    block = iota((blocks, share), 0)
    point = iota((blocks, share), 1)
    own = point // BLK == block
    counts = jnp.broadcast_to(counts_ref[0], (8, blocks)).astype(F32).astype(BF16)
    fill = mm(counts, jnp.where(own, 1.0, 0.0).astype(BF16))[:1].astype(I32)
    usable = point[:1] % BLK < fill
    bias_ref[0] = jnp.where(usable, 0.0, NEGATIVE)
    chosen = jnp.where(own & usable, 1.0, 0.0)
    count = jnp.sum(chosen, axis=1, keepdims=True)
    pooled_ref[0] = (mm(chosen.astype(BF16), kv) / count).astype(BF16)


def first_projection(points, counts, weight):
    balls, share, width = points.shape
    blocks = share // BLK
    ball = lambda rows, cols: pl.BlockSpec((1, rows, cols), lambda b: (b, 0, 0))
    return pl.pallas_call(
        functools.partial(first_projection_kernel, width),
        grid=(balls,),
        in_specs=[ball(share, width), ball(1, blocks), whole(weight)],
        out_specs=[
            ball(share, width), ball(share, 2 * width), ball(blocks, 2 * width), ball(1, share),
        ],
        out_shape=[
            jax.ShapeDtypeStruct((balls, share, width), BF16),
            jax.ShapeDtypeStruct((balls, share, 2 * width), BF16),
            jax.ShapeDtypeStruct((balls, blocks, 2 * width), BF16),
            jax.ShapeDtypeStruct((balls, 1, share), F32),
        ],
        compiler_params=params(),
        cost_estimate=pl.CostEstimate(
            flops=2 * balls * share * width * 3 * width, bytes_accessed=8 * balls * share * width,
            transcendentals=0,
        ),
        name="first_projection",
    )(points, counts.reshape(balls, 1, blocks), weight)


def first_attention_kernel(
    width, shares, query_ref, kv_ref, bias_ref, points_ref, out_ref, *refs
):
    coarse_refs = refs[:shares]
    layer_ref, normed_ref, attended = refs[-3:]
    share = points_ref.shape[1]
    tile = min(2 * TILE, share)
    bias = bias_ref[0]

    def one_pair(pair, carry):
        at = pl.multiple_of(pair * LANES, LANES)
        value_at = pl.multiple_of(width + pair * LANES, LANES)
        keys, values = kv_ref[0, :, pl.ds(at, LANES)], kv_ref[0, :, pl.ds(value_at, LANES)]
        coarse_keys = [ref[0, :, pl.ds(at, LANES)] for ref in coarse_refs]
        coarse_values = [ref[0, :, pl.ds(value_at, LANES)] for ref in coarse_refs]
        for row in range(0, share, tile):
            query = query_ref[0, pl.ds(row, tile), pl.ds(at, LANES)]
            lane = iota(query.shape, 1)
            results = []
            for head in range(2):
                own = own_half(lane, head)
                q = jnp.where(own, query, jnp.zeros_like(query))
                results.append(
                    softmax_mix(
                        [mm_t(q, keys) + bias] + [mm_t(q, part) for part in coarse_keys],
                        [values] + coarse_values,
                    )
                )
            mixture = jnp.where(own_half(lane, 0), results[0], results[1])
            attended[pl.ds(row, tile), pl.ds(at, LANES)] = mixture.astype(BF16)
        return carry

    lax.fori_loop(0, width // LANES, one_pair, 0)
    layer = points_ref[0].astype(F32) + mm(attended[...], out_ref[...])
    layer = layer.astype(BF16)
    layer_ref[0] = layer
    normed_ref[0] = normalize(layer.astype(F32))


def first_attention(index, query, kv, coarse, bias, points, weight, earlier):
    balls, share, width = points.shape
    coarse_rows = sum(part.shape[1] for part in coarse)
    ball = lambda rows, cols: pl.BlockSpec((1, rows, cols), lambda _: (index, 0, 0))
    return pl.pallas_call(
        functools.partial(first_attention_kernel, width, len(coarse)),
        grid=(1,),
        in_specs=[
            ball(share, width), ball(share, 2 * width), ball(1, share), ball(share, width),
            whole(weight),
        ] + [ball(part.shape[1], 2 * width) for part in coarse]
        + [pl.BlockSpec(memory_space=pl.ANY)] * len(earlier),
        out_specs=[ball(share, width), ball(share, width)],
        out_shape=[jax.ShapeDtypeStruct((balls, share, width), BF16)] * 2,
        input_output_aliases={5 + len(coarse) + i: i for i in range(len(earlier))},
        scratch_shapes=[pltpu.VMEM((share, width), BF16)],
        compiler_params=params(),
        cost_estimate=pl.CostEstimate(
            flops=16 * share * (share + coarse_rows) * width,
            bytes_accessed=16 * share * width,
            transcendentals=HEADS * share * (share + coarse_rows),
        ),
        name="first_attention",
    )(query, kv, bias, points, weight, *coarse, *earlier)


def pack_kernel(route_index, offset, slots_ref, rows_ref, packed_ref):
    step = packed_ref.shape[0]
    target = offset + pl.program_id(0) * step + iota((step, rows_ref.shape[0]), 0)
    slot = point_row(slots_ref[route_index : route_index + 1, :])
    chosen = jnp.where(target == slot, 1.0, 0.0).astype(BF16)
    packed_ref[...] = mm(chosen, rows_ref[...]).astype(BF16)


def pack(slots, route_index, rows, packed_rows, offset=0):
    count, width = rows.shape
    step = min(2 * TILE, packed_rows)
    return pl.pallas_call(
        functools.partial(pack_kernel, route_index, offset),
        grid=(packed_rows // step,),
        in_specs=[whole(slots), whole(rows)],
        out_specs=pl.BlockSpec((step, width), lambda t: (t, 0)),
        out_shape=jax.ShapeDtypeStruct((packed_rows, width), BF16),
        compiler_params=params(),
        cost_estimate=pl.CostEstimate(
            flops=2 * packed_rows * width * count, bytes_accessed=4 * packed_rows * width,
            transcendentals=0,
        ),
        name="pack",
    )(slots, rows)


def arrange_kernel(parts, begin, factor, which, limits_ref, *refs):
    rows_refs, place_refs = refs[:parts], refs[parts : 2 * parts]
    weight_ref, out_ref = refs[2 * parts :]
    tile = out_ref.shape[0]
    first = pl.program_id(0) * tile

    @pl.when(first < limits_ref[0, which])
    def _():
        normed = None
        for rows_ref, place_ref in zip(rows_refs, place_refs):
            target = first + iota((tile, place_ref.shape[1]), 0)
            chosen = jnp.where(target == place_ref[...], 1.0, 0.0).astype(BF16)
            part = mm(chosen, rows_ref[...])
            normed = part if normed is None else normed + part
        weight = weight_ref[:, begin : begin + out_ref.shape[1]]
        product = mm(normed.astype(BF16), weight)
        out_ref[...] = (product * factor if factor else product).astype(BF16)

    @pl.when(first >= limits_ref[0, which])
    def _():
        out_ref[...] = jnp.zeros_like(out_ref)


def arrange(limits, which, parts, weight, columns, factor, sorted_rows):
    width = weight.shape[0]
    begin, size = columns
    tile = min(2 * TILE, sorted_rows)
    rows_in = [rows for rows, _ in parts]
    places = [place for _, place in parts]
    count = sum(rows.shape[0] for rows in rows_in)
    return pl.pallas_call(
        functools.partial(arrange_kernel, len(parts), begin, factor, which),
        grid=(sorted_rows // tile,),
        in_specs=[pl.BlockSpec(memory_space=pltpu.SMEM)]
        + [whole(array) for array in rows_in + places]
        + [whole(weight)],
        out_specs=pl.BlockSpec((tile, size), lambda t: (t, 0)),
        out_shape=jax.ShapeDtypeStruct((sorted_rows, size), BF16),
        compiler_params=params(),
        cost_estimate=pl.CostEstimate(
            flops=2 * sorted_rows * (width * count + width * size),
            bytes_accessed=8 * sorted_rows * width, transcendentals=0,
        ),
        name="arrange",
    )(limits, *rows_in, *places, weight)


def rotated_attention_kernel(
    tile, limits_ref, bounds_ref, place_ref, query_ref, key_ref, value_ref, mixture_ref,
    attended, marked,
):
    query_rows, key_rows = query_ref.shape[0], key_ref.shape[0]
    pairs = query_ref.shape[1] // LANES
    together = 2 - pairs % 2

    def inside(rows, first, which):
        row = first + iota((rows, LANES), 0)
        return (row >= bounds_ref[which : which + 1, :]) & (row < bounds_ref[which + 1 : which + 2, :])

    for first in range(0, key_rows, tile):
        span = pl.ds(first, tile)
        closed = jnp.where(inside(tile, first, 2), 0.0, NEGATIVE).astype(BF16)
        lane = iota((tile, LANES), 1)
        for pair in range(pairs):
            lanes = pl.ds(pair * LANES, LANES)
            keys = key_ref[span, lanes]
            for head in range(2):
                marked[head, span, lanes] = jnp.where(own_half(lane, head), keys, closed)

    def attend(index, first_key, keys, pair):
        lanes = pl.ds(pl.multiple_of(pair * LANES, LANES), LANES)
        rows = pl.ds(pl.multiple_of(index * tile, tile), tile)
        span = pl.ds(pl.multiple_of(first_key, tile), keys)
        query = query_ref[rows, lanes]
        values = value_ref[span, lanes]
        label = jnp.where(inside(tile, index * tile, 0), 1.0, 0.0).astype(BF16)
        lane = iota(query.shape, 1)
        results = []
        for head in range(2):
            q = jnp.where(own_half(lane, head), query, label)
            results.append(softmax_mix([mm_t(q, marked[head, span, lanes])], [values]))
        mixture = jnp.where(own_half(lane, 0), results[0], results[1])
        attended[rows, lanes] = mixture.astype(BF16)

    def one_query_tile(index, carry):
        first_key, tiles = limits_ref[index, 0] * tile, limits_ref[index, 1]

        @pl.when(tiles == 0)
        def _():
            rows = pl.ds(pl.multiple_of(index * tile, tile), tile)
            attended[rows, :] = jnp.zeros((tile, attended.shape[1]), BF16)

        for count in range(1, key_rows // tile + 1):

            @pl.when(tiles == count)
            def _(count=count):
                def some_pairs(step, inner):
                    for pair in range(together):
                        attend(index, first_key, count * tile, step * together + pair)
                    return inner

                lax.fori_loop(0, pairs // together, some_pairs, 0)

        return carry

    lax.fori_loop(0, query_rows // tile, one_query_tile, 0)

    def one_tile(index, carry):
        at = pl.multiple_of(index * tile, tile)
        place = place_ref[pl.ds(at, tile), :]
        chosen = jnp.where(iota((tile, query_rows), 1) == place, 1.0, 0.0).astype(BF16)
        mixture_ref[pl.ds(at, tile), :] = mm(chosen, attended[...]).astype(BF16)
        return carry

    lax.fori_loop(0, query_rows // tile, one_tile, 0)


def rotated_attention(limits, bounds, place_column, query, kv, tile, group, groups):
    rows, width = query.shape
    key_rows = kv.shape[0]
    columns = width // groups
    part = lambda size, offset: pl.BlockSpec((size, columns), lambda _: (0, offset + group))
    return pl.pallas_call(
        functools.partial(rotated_attention_kernel, tile),
        grid=(1,),
        in_specs=[
            pl.BlockSpec(memory_space=pltpu.SMEM), whole(bounds), whole(place_column),
            part(rows, 0), part(key_rows, 0), part(key_rows, groups),
        ],
        out_specs=pl.BlockSpec((rows, columns), lambda _: (0, 0)),
        out_shape=jax.ShapeDtypeStruct((rows, columns), BF16),
        scratch_shapes=[
            pltpu.VMEM((rows, columns), BF16), pltpu.VMEM((2, key_rows, columns), BF16),
        ],
        compiler_params=params(),
        cost_estimate=pl.CostEstimate(
            flops=8 * rows * key_rows * columns, bytes_accessed=10 * rows * columns,
            transcendentals=rows * key_rows * HEADS // (2 * groups),
        ),
        name="rotated_attention",
    )(limits, bounds, place_column, query, kv, kv)


def finish_kernel(route_index, parts, slots_ref, layer_ref, weight_ref, *refs):
    returned, result_ref, all_slots = refs[:-2], refs[-2], refs[-1]
    share = layer_ref.shape[1]
    columns = returned[0].shape[1]

    @pl.when(pl.program_id(0) == 0)
    def _():
        all_slots[...] = point_column(slots_ref[route_index : route_index + 1, :])

    slot = all_slots[pl.ds(pl.multiple_of(pl.program_id(0) * share, share), share), :]
    chosen, first = [], 0
    for part in range(parts):
        rows = returned[part].shape[0]
        target = first + iota((share, rows), 1)
        chosen.append(jnp.where(target == slot, 1.0, 0.0).astype(BF16))
        first += rows
    total = layer_ref[0].astype(F32)
    for group in range(len(returned) // parts):
        attended = None
        for part in range(parts):
            found = mm(chosen[part], returned[group * parts + part][...])
            attended = found if attended is None else attended + found
        total = total + mm(attended.astype(BF16), weight_ref[pl.ds(group * columns, columns), :])
    result_ref[0] = total.astype(BF16)


def finish(slots, route_index, layer, weight, returned):
    balls, share, width = layer.shape
    ball = lambda rows, cols: pl.BlockSpec((1, rows, cols), lambda b: (b, 0, 0))
    flat = [part for parts in returned for part in parts]
    rows = sum(part.shape[0] for part in returned[0])
    return pl.pallas_call(
        functools.partial(finish_kernel, route_index, len(returned[0])),
        grid=(balls,),
        in_specs=[whole(slots), ball(share, width), whole(weight)]
        + [whole(part) for part in flat],
        out_specs=ball(share, width),
        out_shape=jax.ShapeDtypeStruct(layer.shape, BF16),
        scratch_shapes=[pltpu.VMEM((balls * share, 1), I32)],
        compiler_params=params(),
        cost_estimate=pl.CostEstimate(
            flops=2 * balls * share * width * (rows + width),
            bytes_accessed=8 * balls * share * width, transcendentals=0,
        ),
        name="finish",
    )(slots, layer, weight, *flat)


def side_by_side(mine, other, lower, axis):
    return jnp.where(
        lower, jnp.concatenate([mine, other], axis=axis), jnp.concatenate([other, mine], axis=axis)
    )


def double(array, axis_name, step, axis):
    count = lax.axis_size(axis_name)
    other = lax.ppermute(array, axis_name, [(i, i ^ step) for i in range(count)])
    return side_by_side(array, other, (lax.axis_index(axis_name) & step) == 0, axis)


def gather_shares(array, axis_name, axis):
    count = lax.axis_size(axis_name)
    if count & (count - 1):
        return lax.all_gather(array, axis_name, axis=axis, tiled=True)
    step = 1
    while step < count:
        array = double(array, axis_name, step, axis)
        step *= 2
    return array


def exchange(rows, wide_count):
    parts = rows.reshape((wide_count, rows.shape[0] // wide_count) + rows.shape[1:])
    parts = lax.all_to_all(parts, "wide", split_axis=0, concat_axis=0, tiled=True)
    return parts.reshape(rows.shape)


def earlier_sum(values):
    return jnp.cumsum(values, axis=-1, dtype=I32) - values


def sorted_places(label, fill, own_blocks, labels, key_parts, tile):
    member = (label[None, :] == jnp.arange(labels, dtype=I32)[:, None]).astype(I32)
    own = member[:, :own_blocks]
    own_total = jnp.sum(own, axis=1, dtype=I32)
    own_start = earlier_sum(own_total)
    own_end = own_start + own_total
    query_at = jnp.sum(own * (own_start[:, None] + earlier_sum(own)), axis=0, dtype=I32)
    query_place = jnp.where(
        label[:own_blocks, None] >= 0,
        query_at[:, None] * BLK + jnp.arange(BLK, dtype=I32)[None, :],
        -1,
    ).reshape(-1)
    usable = member * fill[None, :]
    key_total = jnp.sum(usable, axis=1, dtype=I32)
    key_start = earlier_sum(key_total)
    key_end = key_start + key_total
    key_at = jnp.sum(member * (key_start[:, None] + earlier_sum(usable)), axis=0, dtype=I32)
    point = jnp.arange(BLK, dtype=I32)[None, :]
    key_place = jnp.where(point < fill[:, None], key_at[:, None] + point, -1).reshape(-1)
    tiles = own_blocks * BLK // tile
    first = jnp.arange(tiles, dtype=I32)[:, None] * tile
    meets = (own_start[None, :] * BLK < first + tile) & (own_end[None, :] * BLK > first)
    meets = meets & (own_total[None, :] > 0)
    low = jnp.min(jnp.where(meets, key_start[None, :], label.shape[0] * BLK), axis=1)
    high = jnp.max(jnp.where(meets, key_end[None, :], 0), axis=1)
    low_tile = low // tile
    count = jnp.where(high > 0, (high + tile - 1) // tile - low_tile, 0)
    live = [jnp.broadcast_to(jnp.sum(total), count.shape) for total in (own_total * BLK, key_total)]
    limits = jnp.stack([jnp.where(high > 0, low_tile, 0), count] + live, axis=1)
    bounds = jnp.stack([own_start * BLK, own_end * BLK, key_start, key_end])
    bounds = jnp.pad(bounds, ((0, 4), (0, LANES // 2 - labels)))
    bounds = jnp.concatenate([bounds, bounds], axis=1)
    key_places = [part.reshape(1, -1) for part in jnp.split(key_place, key_parts)]
    return query_place.reshape(1, -1), query_place.reshape(-1, 1), key_places, limits, bounds


def labels_at(position, values, count):
    at = position[:, None, :] == jnp.arange(count, dtype=I32)[None, :, None]
    return jnp.sum(jnp.where(at, values[:, None, :], 0), axis=-1, dtype=I32)


def second_attention(places, own_rows, key_parts, weight, groups):
    query_row, query_column, key_rows, limits, bounds = places
    rows, width = own_rows.shape
    tile = min(TILE, rows)
    factor = math.log2(math.e) / math.sqrt(width // HEADS)
    query = arrange(limits, 2, [(own_rows, query_row)], weight, (0, width), factor, rows)
    parts = list(zip(key_parts, key_rows))
    kv = arrange(limits, 3, parts, weight, (width, 2 * width), None, rows * len(parts))
    for group in range(groups):
        yield rotated_attention(limits, bounds, query_column, query, kv, tile, group, groups)


def by_slots(normed, slots_of, route_index, codes, index, capacity, weight, groups):
    wide_count = codes.shape[0]
    slots = wide_count * capacity
    packed, codes = lax.optimization_barrier((pack(slots_of, route_index, normed, slots * BLK), codes))
    arrived = exchange(packed, wide_count)
    mine = (codes // (2 * BLK)) == index
    rank = jnp.where(mine, earlier_sum(mine.astype(I32)), -1)
    found = labels_at(rank, codes % (2 * BLK) + 1, capacity).reshape(slots)
    live = found > 0
    label = jnp.where(live, (found - 1) // BLK, -1)
    fill = jnp.where(live, (found - 1) % BLK + 1, 0)
    places = sorted_places(label, fill, slots, 2, 1, min(TILE, slots * BLK))
    mixtures = second_attention(places, arrived, [arrived], weight, groups)
    return [[exchange(mixture, wide_count)] for mixture in mixtures]


def lower_mask(size):
    return jnp.where(iota((size, size), 0) < iota((size, size), 1), 1.0, 0.0).astype(BF16)


def ones_where(condition):
    return jnp.where(condition, 1.0, 0.0).astype(BF16)


def to_row(column):
    size = column.shape[0]
    same = iota((size, size), 0) == iota((size, size), 1)
    return jnp.sum(jnp.where(same, column, 0.0), axis=0, keepdims=True)


def route_kernel(
    wide_count, capacity, unit, here_ref, codes_ref, starts_ref, slots_ref, fits_ref
):
    devices, block_count = codes_ref.shape
    lane = iota((1, LANES), 1)
    destination = codes_ref[...] // (2 * BLK)
    worst = jnp.zeros((1, LANES), F32)
    for side in range(2):
        part = destination[side * wide_count : (side + 1) * wide_count]
        held = jnp.zeros((wide_count, LANES), F32)
        for d in range(wide_count):
            count = jnp.sum(jnp.where(part == d, 1.0, 0.0), axis=1, keepdims=True)
            held = jnp.where(lane == d, count, held)
        load = jnp.sum(held, axis=0, keepdims=True)
        starts = jnp.zeros((wide_count, LANES), F32)
        for d in range(wide_count):
            other = load[:, d : d + 1]
            earlier = (other > load) | ((other == load) & (d < lane))
            starts = starts + jnp.where(earlier, held[:, d : d + 1], 0.0)
        starts_ref[pl.ds(side * wide_count, wide_count), :] = starts
        run = jnp.floor(starts * (1.0 / unit))
        last = jnp.floor((starts + held - 1.0) * (1.0 / unit))
        low = jnp.min(jnp.where(held > 0.0, run, 1e6), axis=0, keepdims=True)
        high = jnp.max(jnp.where(held > 0.0, last, -1.0), axis=0, keepdims=True)
        worst = jnp.maximum(worst, jnp.where((high > low) & (lane < wide_count), 1.0, 0.0))
    fits_ref[...] = jnp.broadcast_to(jnp.max(worst, axis=1, keepdims=True), (8, LANES)).astype(I32)

    core = here_ref[0]
    index = core * wide_count + here_ref[1]
    own = codes_ref[pl.ds(index, 1), :] // (2 * BLK)
    start = starts_ref[pl.ds(index, 1), :]
    member = own == iota((wide_count, block_count), 0)
    rank = mm(ones_where(member), lower_mask(block_count))
    rank = jnp.sum(jnp.where(member, rank, 0.0), axis=0, keepdims=True)
    place = rank
    for d in range(wide_count):
        place = place + jnp.where(own == d, start[:, d : d + 1], 0.0)
    place = place.astype(I32)
    run, within = place // unit, place % unit
    half = unit // 2
    away = (within // half != core).astype(I32)
    slots_ref[0:1, :] = away * (block_count // 2) + run * half + within % half
    slots_ref[1:2, :] = own * capacity + rank.astype(I32)


def route(codes, here, capacity, unit):
    sides, wide_count, block_count = codes.shape
    flat = codes.reshape(sides * wide_count, block_count)
    full = lambda shape: pl.BlockSpec(shape, lambda _: (0, 0))
    return pl.pallas_call(
        functools.partial(route_kernel, wide_count, capacity, unit),
        grid=(1,),
        in_specs=[pl.BlockSpec(memory_space=pltpu.SMEM), whole(flat)],
        out_specs=[full((sides * wide_count, LANES)), full((8, block_count)), full((8, LANES))],
        out_shape=[
            jax.ShapeDtypeStruct((sides * wide_count, LANES), F32),
            jax.ShapeDtypeStruct((8, block_count), I32),
            jax.ShapeDtypeStruct((8, LANES), I32),
        ],
        compiler_params=params(),
        name="route",
    )(here, flat)


def plan_kernel(
    unit, tile, here_ref, codes_ref, starts_ref,
    query_row_ref, query_column_ref, own_key_ref, other_key_ref, limits_ref, bounds_ref,
):
    _, wide_count, block_count = codes_ref.shape
    half = unit // 2
    blocks = wide_count * half
    core, side, base = here_ref[0], here_ref[1] % 2, here_ref[1] // 2 * unit
    codes = codes_ref[side]
    destination = codes // (2 * BLK)
    members = jnp.concatenate([ones_where(destination == d) for d in range(wide_count)], axis=0)
    rank = mm(members, lower_mask(block_count))
    starts = starts_ref[pl.ds(pl.multiple_of(side * wide_count, wide_count), wide_count), :]
    position = jnp.zeros(codes.shape, F32)
    for d in range(wide_count):
        at = starts[:, d : d + 1] + rank[d * wide_count : (d + 1) * wide_count]
        position = position + jnp.where(destination == d, at, 0.0)
    position = position.astype(I32) - base
    values = codes.astype(F32)

    def labels_of(which):
        columns = []
        for source in range(wide_count):
            at = iota((half, block_count), 0) + which * half == position[source : source + 1]
            found = jnp.where(at, values[source : source + 1], 0.0)
            columns.append(jnp.sum(found, axis=1, keepdims=True))
        found = to_row(jnp.concatenate(columns, axis=0)).astype(I32)
        member = found // BLK == iota((LANES, blocks), 0) % (LANES // 2)
        return member, found % BLK + 1

    earlier = lower_mask(blocks)
    below = iota((LANES, LANES), 1) < iota((LANES, LANES), 0) % (LANES // 2)

    def begin(total):
        return jnp.sum(jnp.where(below, to_row(total), 0.0), axis=1, keepdims=True)

    def place_of(member, at):
        once = member & (iota(member.shape, 0) < LANES // 2)
        return jnp.sum(jnp.where(once, at, 0.0), axis=0, keepdims=True).astype(I32)

    own, own_fill = labels_of(core)
    other, other_fill = labels_of(1 - core)
    own_ones = ones_where(own)
    own_total = jnp.sum(jnp.where(own, 1.0, 0.0), axis=1, keepdims=True)
    own_start = begin(own_total)
    query = place_of(own, own_start + mm(own_ones, earlier))
    query_row_ref[...] = point_row(query)
    query_column_ref[...] = point_column(query)

    fills = [jnp.where(m, f.astype(F32), 0.0) for m, f in ((own, own_fill), (other, other_fill))]
    totals = [jnp.sum(f, axis=1, keepdims=True) for f in fills]
    key_start = begin(totals[0] + totals[1])
    key_end = key_start + totals[0] + totals[1]
    ranks = [mm(f.astype(BF16), earlier) for f in fills]
    spread = ones_where(iota((blocks, blocks * BLK), 1) // BLK == iota((blocks, blocks * BLK), 0))
    point = iota((1, blocks * BLK), 1) % BLK
    for ref, at, fill in (
        (own_key_ref, place_of(own, key_start + ranks[0]), own_fill),
        (other_key_ref, place_of(other, key_start + totals[0] + ranks[1]), other_fill),
    ):
        digits = jnp.concatenate([at // 32, at % 32, fill] + [jnp.zeros_like(at)] * 5, axis=0)
        digits = mm(digits.astype(F32).astype(BF16), spread).astype(I32)
        ref[...] = jnp.where(point < digits[2:3], digits[:1] * 32 + digits[1:2] + point, -1)

    rows = [to_row(c) for c in (own_start * BLK, (own_start + own_total) * BLK, key_start, key_end)]
    bounds_ref[...] = jnp.concatenate(rows + [jnp.zeros_like(rows[0])] * 4, axis=0).astype(I32)
    first = (iota((8, LANES), 0) * tile).astype(F32)
    meets = (rows[0] < first + tile) & (rows[1] > first) & (rows[1] > rows[0])
    low = jnp.min(jnp.where(meets, rows[2], 1e6), axis=1, keepdims=True).astype(I32)
    high = jnp.max(jnp.where(meets, rows[3], 0.0), axis=1, keepdims=True).astype(I32)
    low_tile = low // tile
    count = (high + tile - 1) // tile - low_tile
    live = jnp.max(rows[3], axis=1, keepdims=True).astype(I32)
    lane = iota((8, LANES), 1)
    limits = jnp.where(lane == 0, low_tile, jnp.where(lane == 1, count, 0))
    limits = jnp.where(lane == 2, blocks * BLK, jnp.where(lane == 3, live, limits))
    limits_ref[...] = jnp.where((lane < 2) & (high <= 0), 0, limits)


def plan(here, codes, starts, unit, tile):
    wide_count = codes.shape[1]
    rows = wide_count * unit // 2 * BLK
    shapes = [(1, rows), (rows, 1), (1, rows), (1, rows), (8, LANES), (8, LANES)]
    full = lambda shape: pl.BlockSpec(shape, lambda _: (0, 0))
    outs = pl.pallas_call(
        functools.partial(plan_kernel, unit, tile),
        grid=(1,),
        in_specs=[pl.BlockSpec(memory_space=pltpu.SMEM), whole(codes), whole(starts)],
        out_specs=[full(shape) for shape in shapes],
        out_shape=[jax.ShapeDtypeStruct(shape, I32) for shape in shapes],
        compiler_params=params(),
        cost_estimate=pl.CostEstimate(flops=1 << 33, bytes_accessed=1 << 22, transcendentals=0),
        name="plan",
    )(here, codes, starts)
    return outs[0], outs[1], outs[2:4], outs[4], outs[5]


def by_chips(normed, slots, here, codes, starts, weight, groups):
    _, wide_count, block_count = codes.shape
    unit = 2 * block_count // wide_count
    units = wide_count // 2
    rows_half = block_count * BLK // 2
    swap = lambda array: lax.ppermute(array, "narrow", [(0, 1), (1, 0)])
    is_first = lax.axis_index("narrow") == 0

    def pair_up(kept, taken):
        low = jnp.where(is_first, kept, taken).reshape(units, 1, rows_half // units, -1)
        high = jnp.where(is_first, taken, kept).reshape(units, 1, rows_half // units, -1)
        return jnp.concatenate([low, high], axis=1).reshape(2 * rows_half, -1)

    def take_apart(array):
        both = array.reshape(units, 2, rows_half // units, -1)
        low, high = both[:, 0].reshape(rows_half, -1), both[:, 1].reshape(rows_half, -1)
        return jnp.where(is_first, low, high), jnp.where(is_first, high, low)

    taken = swap(pack(slots, 0, normed, rows_half, rows_half))
    kept = pack(slots, 0, normed, rows_half)
    arrived = exchange(pair_up(kept, taken), wide_count)
    places = plan(here, codes, starts, unit, min(TILE, 2 * rows_half))
    mixtures = second_attention(places, arrived, [arrived, swap(arrived)], weight, groups)
    returned = []
    for mixture in mixtures:
        kept, given = take_apart(exchange(mixture, wide_count))
        returned.append([kept, swap(given)])
    return returned


def on_device(
    points, counts, destination, rotated_ball, qkv_first, out_first, qkv_second, out_second
):
    balls, share, width = points.shape
    wide_count, narrow_count = lax.axis_size("wide"), lax.axis_size("narrow")
    block_count = destination.size
    capacity = max(2, 2 * block_count // wide_count)
    groups = 1

    flat = (block_count,)
    dest_flat = destination.reshape(flat)
    code = (dest_flat * 2 + rotated_ball.reshape(flat)) * BLK + counts.reshape(flat) - 1
    power = not wide_count & (wide_count - 1)
    paired = narrow_count == 2 and power and wide_count > 1 and 2 * wide_count <= LANES // 2
    paired = paired and block_count % wide_count == 0 and capacity * wide_count == 2 * block_count
    paired = paired and TILE <= block_count * BLK <= 8 * TILE and block_count % TILE == 0

    codes = code.reshape(1, 1, block_count)
    if paired:
        cores = [(0, 1), (1, 0)]
        chips = [(i, i ^ 1) for i in range(wide_count)]
        both = [(i, i ^ 3) for i in range(2 * wide_count)]
        mine = (codes, lax.ppermute(codes, "narrow", cores))
        theirs = (
            lax.ppermute(codes, "wide", chips), lax.ppermute(codes, ("wide", "narrow"), both)
        )
        lower = lax.axis_index("narrow") == 0
        codes = side_by_side(
            side_by_side(*mine, lower, 0), side_by_side(*theirs, lower, 0),
            (lax.axis_index("wide") & 1) == 0, 1,
        )
    elif power:
        codes = double(codes, "wide", 1, 1)
    query, kv, pooled, bias = first_projection(points, counts, qkv_first)
    if narrow_count == 2:
        coarse = [pooled, lax.ppermute(pooled, "narrow", [(0, 1), (1, 0)])]
    else:
        coarse = [gather_shares(pooled, "narrow", 1)]
    results = ()
    step = 2
    if power and step < wide_count:
        codes = double(codes, "wide", step, 1)
        step *= 2
    for ball in range(balls):
        if power:
            while step < wide_count and (step < 8 << ball or ball == balls - 1):
                coarse, codes = lax.optimization_barrier((coarse, codes))
                codes = double(codes, "wide", step, 1)
                step *= 2
        results = first_attention(ball, query, kv, coarse, bias, points, out_first, results)
    if not power:
        codes = gather_shares(codes, "wide", 1)
    layer_one, normed = results
    normed = normed.reshape(balls * share, width)

    def slot_route(codes, slots, route_index):
        index = lax.axis_index("wide")
        returned = by_slots(normed, slots, route_index, codes, index, capacity, qkv_second, groups)
        return finish(slots, route_index, layer_one, out_second, returned)

    if not paired:
        onehot = (jnp.arange(wide_count, dtype=I32)[:, None] == dest_flat[None, :]).astype(I32)
        rank = jnp.sum(earlier_sum(onehot) * onehot, axis=0, dtype=I32)
        return slot_route(codes[0], (dest_flat * capacity + rank).reshape(1, -1), 0)

    core = lax.axis_index("narrow")
    here = jnp.stack([core, lax.axis_index("wide")]).astype(I32)
    starts, slots, worst = route(codes, here, capacity, 2 * block_count // wide_count)
    def chip_route():
        returned = by_chips(normed, slots, here, codes, starts, qkv_second, groups)
        return finish(slots, 0, layer_one, out_second, returned)

    return lax.cond(worst[0, 0] == 0, chip_route, lambda: slot_route(codes[core], slots, 1))


def solution(mesh):
    split = P("wide", "narrow")
    in_specs = (P("wide", "narrow", None), split, split, split, P(), P(), P(), P())
    out_specs = P("wide", "narrow", None)
    return jax.shard_map(
        on_device, mesh=mesh, in_specs=in_specs, out_specs=out_specs, check_vma=False
    )
```

```python
import functools
import math

import jax
import jax.numpy as jnp
from jax import lax
from jax.experimental import pallas as pl
from jax.experimental.pallas import tpu as pltpu
from jax.sharding import PartitionSpec as P

HEADS = 8
BLK = 4
EPSILON = 1e-06
NEGATIVE = -1e30
LANES = 128
TILE = 256
VMEM_LIMIT = 56 * 1024 * 1024
BF16 = jnp.bfloat16
F32 = jnp.float32
I32 = jnp.int32

NT = (((1,), (1,)), ((), ()))


def iota(shape, axis):
    return lax.broadcasted_iota(I32, shape, axis)


def mm(left, right):
    return jnp.dot(left, right, preferred_element_type=F32)


def mm_t(left, right):
    return lax.dot_general(left, right, NT, preferred_element_type=F32)


def params():
    return pltpu.CompilerParams(vmem_limit_bytes=VMEM_LIMIT)


def whole(array):
    return pl.BlockSpec(array.shape, lambda *_: (0,) * len(array.shape))


def normalize(rows):
    return (rows * lax.rsqrt(jnp.mean(rows * rows, axis=-1, keepdims=True) + EPSILON)).astype(BF16)


def project_rows(normed, weight, width):
    factor = math.log2(math.e) / math.sqrt(width // HEADS)
    query = (mm(normed, weight[:, :width]) * factor).astype(BF16)
    return query, mm(normed, weight[:, width:]).astype(BF16)


def block_digits(values):
    digits = jnp.concatenate([values // 32, values % 32] + [jnp.zeros_like(values)] * 6, axis=0)
    return digits.astype(F32).astype(BF16)


def point_row(values):
    blocks = values.shape[1]
    spread = iota((blocks, blocks * BLK), 1) // BLK == iota((blocks, blocks * BLK), 0)
    digits = mm(block_digits(values), jnp.where(spread, 1.0, 0.0).astype(BF16)).astype(I32)
    return (digits[:1] * 32 + digits[1:2]) * BLK + iota((1, blocks * BLK), 1) % BLK


def point_column(values):
    blocks = values.shape[1]
    spread = iota((blocks * BLK, blocks), 0) // BLK == iota((blocks * BLK, blocks), 1)
    digits = mm_t(jnp.where(spread, 1.0, 0.0).astype(BF16), block_digits(values)).astype(I32)
    return (digits[:, :1] * 32 + digits[:, 1:2]) * BLK + iota((blocks * BLK, 1), 0) % BLK


def own_half(lane, head):
    return (lane < LANES // 2) if head == 0 else (lane >= LANES // 2)


def softmax_mix(scores, values):
    highest = functools.reduce(jnp.maximum, [jnp.max(s, axis=-1, keepdims=True) for s in scores])
    total = None
    for s, v in zip(scores, values):
        wide = jnp.concatenate([v, jnp.ones_like(v)], axis=1)
        part = mm(jnp.exp2(s - highest).astype(BF16), wide)
        total = part if total is None else total + part
    return total[:, :LANES] / total[:, LANES:]


def first_projection_kernel(
    width, points_ref, counts_ref, weight_ref, query_ref, kv_ref, pooled_ref, bias_ref
):
    normed = normalize(points_ref[0].astype(F32))
    query, kv = project_rows(normed, weight_ref, width)
    query_ref[0] = query
    kv_ref[0] = kv
    share = normed.shape[0]
    blocks = share // BLK
    block = iota((blocks, share), 0)
    point = iota((blocks, share), 1)
    own = point // BLK == block
    counts = jnp.broadcast_to(counts_ref[0], (8, blocks)).astype(F32).astype(BF16)
    fill = mm(counts, jnp.where(own, 1.0, 0.0).astype(BF16))[:1].astype(I32)
    usable = point[:1] % BLK < fill
    bias_ref[0] = jnp.where(usable, 0.0, NEGATIVE)
    chosen = jnp.where(own & usable, 1.0, 0.0)
    count = jnp.sum(chosen, axis=1, keepdims=True)
    pooled_ref[0] = (mm(chosen.astype(BF16), kv) / count).astype(BF16)


def first_projection(points, counts, weight):
    balls, share, width = points.shape
    blocks = share // BLK
    ball = lambda rows, cols: pl.BlockSpec((1, rows, cols), lambda b: (b, 0, 0))
    return pl.pallas_call(
        functools.partial(first_projection_kernel, width),
        grid=(balls,),
        in_specs=[ball(share, width), ball(1, blocks), whole(weight)],
        out_specs=[
            ball(share, width), ball(share, 2 * width), ball(blocks, 2 * width), ball(1, share),
        ],
        out_shape=[
            jax.ShapeDtypeStruct((balls, share, width), BF16),
            jax.ShapeDtypeStruct((balls, share, 2 * width), BF16),
            jax.ShapeDtypeStruct((balls, blocks, 2 * width), BF16),
            jax.ShapeDtypeStruct((balls, 1, share), F32),
        ],
        compiler_params=params(),
        cost_estimate=pl.CostEstimate(
            flops=2 * balls * share * width * 3 * width, bytes_accessed=8 * balls * share * width,
            transcendentals=0,
        ),
        name="first_projection",
    )(points, counts.reshape(balls, 1, blocks), weight)


def joined(parts):
    return parts[0] if len(parts) == 1 else jnp.concatenate(parts, axis=0)


def first_attention_kernel(
    width, shares, query_ref, kv_ref, bias_ref, points_ref, out_ref, *refs
):
    coarse_refs = refs[:shares]
    layer_ref, normed_ref, attended = refs[-3:]
    share = points_ref.shape[1]
    tile = min(2 * TILE, share)
    bias = bias_ref[0]

    def one_pair(pair, carry):
        at = pl.multiple_of(pair * LANES, LANES)
        value_at = pl.multiple_of(width + pair * LANES, LANES)
        keys, values = kv_ref[0, :, pl.ds(at, LANES)], kv_ref[0, :, pl.ds(value_at, LANES)]
        coarse_keys = joined([ref[0, :, pl.ds(at, LANES)] for ref in coarse_refs])
        coarse_values = joined([ref[0, :, pl.ds(value_at, LANES)] for ref in coarse_refs])
        for row in range(0, share, tile):
            query = query_ref[0, pl.ds(row, tile), pl.ds(at, LANES)]
            lane = iota(query.shape, 1)
            results = []
            for head in range(2):
                own = own_half(lane, head)
                q = jnp.where(own, query, jnp.zeros_like(query))
                results.append(
                    softmax_mix(
                        [mm_t(q, keys) + bias, mm_t(q, coarse_keys)], [values, coarse_values]
                    )
                )
            mixture = jnp.where(own_half(lane, 0), results[0], results[1])
            attended[pl.ds(row, tile), pl.ds(at, LANES)] = mixture.astype(BF16)
        return carry

    lax.fori_loop(0, width // LANES, one_pair, 0, unroll=4)
    layer = points_ref[0].astype(F32) + mm(attended[...], out_ref[...])
    layer = layer.astype(BF16)
    layer_ref[0] = layer
    normed_ref[0] = normalize(layer.astype(F32))


def first_attention(index, query, kv, coarse, bias, points, weight, earlier):
    balls, share, width = points.shape
    coarse_rows = sum(part.shape[1] for part in coarse)
    ball = lambda rows, cols: pl.BlockSpec((1, rows, cols), lambda _: (index, 0, 0))
    return pl.pallas_call(
        functools.partial(first_attention_kernel, width, len(coarse)),
        grid=(1,),
        in_specs=[
            ball(share, width), ball(share, 2 * width), ball(1, share), ball(share, width),
            whole(weight),
        ] + [ball(part.shape[1], 2 * width) for part in coarse]
        + [pl.BlockSpec(memory_space=pl.ANY)] * len(earlier),
        out_specs=[ball(share, width), ball(share, width)],
        out_shape=[jax.ShapeDtypeStruct((balls, share, width), BF16)] * 2,
        input_output_aliases={5 + len(coarse) + i: i for i in range(len(earlier))},
        scratch_shapes=[pltpu.VMEM((share, width), BF16)],
        compiler_params=params(),
        cost_estimate=pl.CostEstimate(
            flops=16 * share * (share + coarse_rows) * width,
            bytes_accessed=16 * share * width,
            transcendentals=HEADS * share * (share + coarse_rows),
        ),
        name="first_attention",
    )(query, kv, bias, points, weight, *coarse, *earlier)


def pack_kernel(route_index, offset, slots_ref, rows_ref, packed_ref):
    step = packed_ref.shape[0]
    target = offset + pl.program_id(0) * step + iota((step, rows_ref.shape[0]), 0)
    slot = point_row(slots_ref[route_index : route_index + 1, :])
    chosen = jnp.where(target == slot, 1.0, 0.0).astype(BF16)
    packed_ref[...] = mm(chosen, rows_ref[...]).astype(BF16)


def pack(slots, route_index, rows, packed_rows, offset=0):
    count, width = rows.shape
    step = min(2 * TILE, packed_rows)
    return pl.pallas_call(
        functools.partial(pack_kernel, route_index, offset),
        grid=(packed_rows // step,),
        in_specs=[whole(slots), whole(rows)],
        out_specs=pl.BlockSpec((step, width), lambda t: (t, 0)),
        out_shape=jax.ShapeDtypeStruct((packed_rows, width), BF16),
        compiler_params=params(),
        cost_estimate=pl.CostEstimate(
            flops=2 * packed_rows * width * count, bytes_accessed=4 * packed_rows * width,
            transcendentals=0,
        ),
        name="pack",
    )(slots, rows)


def arrange_kernel(factor, limits_ref, rows_ref, place_ref, weight_ref, out_ref):
    tile, width = out_ref.shape
    first = pl.program_id(0) * tile

    @pl.when(first < limits_ref[0, 2])
    def _():
        target = first + iota((tile, place_ref.shape[1]), 0)
        chosen = jnp.where(target == place_ref[...], 1.0, 0.0).astype(BF16)
        normed = mm(chosen, rows_ref[...]).astype(BF16)
        out_ref[...] = (mm(normed, weight_ref[...]) * factor).astype(BF16)

    @pl.when(first >= limits_ref[0, 2])
    def _():
        out_ref[...] = jnp.zeros_like(out_ref)


def arrange(limits, rows, place_row, weight, factor):
    count, width = rows.shape
    tile = min(2 * TILE, count)
    return pl.pallas_call(
        functools.partial(arrange_kernel, factor),
        grid=(count // tile,),
        in_specs=[
            pl.BlockSpec(memory_space=pltpu.SMEM), whole(rows), whole(place_row),
            pl.BlockSpec((width, width), lambda t: (0, 0)),
        ],
        out_specs=pl.BlockSpec((tile, width), lambda t: (t, 0)),
        out_shape=jax.ShapeDtypeStruct((count, width), BF16),
        compiler_params=params(),
        cost_estimate=pl.CostEstimate(
            flops=2 * count * width * (count + width), bytes_accessed=4 * count * width,
            transcendentals=0,
        ),
        name="arrange",
    )(limits, rows, place_row, weight)


def rotated_attention_kernel(
    parts, step, tile, eager, limits_ref, bounds_ref, place_ref, query_ref, weight_ref, *refs
):
    rows_refs, key_places = refs[:parts], refs[parts : 2 * parts]
    mixture_ref, attended, marked, values_all = refs[2 * parts :]
    query_rows, width = query_ref.shape
    key_rows = values_all.shape[0]
    pairs = width // LANES
    portion = min(2 * tile, key_rows)

    def inside(rows, first, which):
        row = first + iota((rows, LANES), 0)
        return (row >= bounds_ref[which : which + 1, :]) & (row < bounds_ref[which + 1 : which + 2, :])

    def make_keys(index, carry):
        first = pl.multiple_of(index * portion, portion)
        span = pl.ds(first, portion)
        normed = None
        for rows_ref, key_place in zip(rows_refs, key_places):
            target = first + iota((portion, key_place.shape[1]), 0)
            chosen = jnp.where(target == key_place[...], 1.0, 0.0).astype(BF16)
            part = mm(chosen, rows_ref[...])
            normed = part if normed is None else normed + part
        normed = normed.astype(BF16)
        keys = mm(normed, weight_ref[:, width : 2 * width]).astype(BF16)
        values_all[span, :] = mm(normed, weight_ref[:, 2 * width :]).astype(BF16)
        closed = jnp.where(inside(portion, first, 2), 0.0, NEGATIVE).astype(BF16)
        lane = iota((portion, LANES), 1)
        for pair in range(pairs):
            at = slice(pair * LANES, (pair + 1) * LANES)
            for head in range(2):
                marked[head, span, at] = jnp.where(own_half(lane, head), keys[:, at], closed)
        return carry

    lax.fori_loop(0, (limits_ref[0, 3] + portion - 1) // portion, make_keys, 0)

    def attend(index, first_key, keys, pair):
        lanes = pl.ds(pl.multiple_of(pair * LANES, LANES), LANES)
        rows = pl.ds(pl.multiple_of(index * step, step), step)
        span = pl.ds(pl.multiple_of(first_key, tile), keys)
        query = query_ref[rows, lanes]
        values = values_all[span, lanes]
        label = jnp.where(inside(step, index * step, 0), 1.0, 0.0).astype(BF16)
        lane = iota(query.shape, 1)
        results = []
        for head in range(2):
            q = jnp.where(own_half(lane, head), query, label)
            results.append(softmax_mix([mm_t(q, marked[head, span, lanes])], [values]))
        mixture = jnp.where(own_half(lane, 0), results[0], results[1])
        attended[rows, lanes] = mixture.astype(BF16)

    def one_query_tile(index, carry):
        first_key, tiles = limits_ref[index, 0] * tile, limits_ref[index, 1]

        @pl.when(tiles == 0)
        def _():
            rows = pl.ds(pl.multiple_of(index * step, step), step)
            attended[rows, :] = jnp.zeros((step, attended.shape[1]), BF16)

        for count in range(1, key_rows // tile + 1):

            @pl.when(tiles == count)
            def _(count=count):
                together = math.gcd(pairs, eager if count * tile <= 6 * TILE else 1)

                def some_pairs(step, inner):
                    for pair in range(together):
                        attend(index, first_key, count * tile, step * together + pair)
                    return inner

                lax.fori_loop(0, pairs // together, some_pairs, 0)

        return carry

    lax.fori_loop(0, query_rows // step, one_query_tile, 0)

    def one_tile(index, carry):
        at = pl.multiple_of(index * step, step)
        place = place_ref[pl.ds(at, step), :]
        chosen = jnp.where(iota((step, query_rows), 1) == place, 1.0, 0.0).astype(BF16)
        mixture_ref[pl.ds(at, step), :] = mm(chosen, attended[...]).astype(BF16)
        return carry

    lax.fori_loop(0, query_rows // step, one_tile, 0)


def rotated_attention(places, query, parts, weight, step, tile, eager):
    _, place_column, key_places, limits, bounds = places
    rows, width = query.shape
    key_rows = sum(part.shape[0] for part in parts)
    return pl.pallas_call(
        functools.partial(rotated_attention_kernel, len(parts), step, tile, eager),
        grid=(1,),
        in_specs=[
            pl.BlockSpec(memory_space=pltpu.SMEM), whole(bounds), whole(place_column),
            whole(query), whole(weight),
        ] + [whole(array) for array in list(parts) + list(key_places)],
        out_specs=pl.BlockSpec((rows, width), lambda _: (0, 0)),
        out_shape=jax.ShapeDtypeStruct((rows, width), BF16),
        scratch_shapes=[
            pltpu.VMEM((rows, width), BF16), pltpu.VMEM((2, key_rows, width), BF16),
            pltpu.VMEM((key_rows, width), BF16),
        ],
        compiler_params=params(),
        cost_estimate=pl.CostEstimate(
            flops=8 * rows * key_rows * width, bytes_accessed=10 * rows * width,
            transcendentals=rows * key_rows * HEADS // 2,
        ),
        name="rotated_attention",
    )(limits, bounds, place_column, query, weight, *parts, *key_places)


def finish_kernel(route_index, slots_ref, layer_ref, weight_ref, *refs):
    returned, result_ref, all_slots = refs[:-2], refs[-2], refs[-1]
    share = layer_ref.shape[1]

    @pl.when(pl.program_id(0) == 0)
    def _():
        all_slots[...] = point_column(slots_ref[route_index : route_index + 1, :])

    slot = all_slots[pl.ds(pl.multiple_of(pl.program_id(0) * share, share), share), :]
    attended, first = None, 0
    for part in returned:
        target = first + iota((share, part.shape[0]), 1)
        found = mm(jnp.where(target == slot, 1.0, 0.0).astype(BF16), part[...])
        attended = found if attended is None else attended + found
        first += part.shape[0]
    layer = layer_ref[0].astype(F32)
    result_ref[0] = (layer + mm(attended.astype(BF16), weight_ref[...])).astype(BF16)


def finish(slots, route_index, layer, weight, returned):
    balls, share, width = layer.shape
    ball = lambda rows, cols: pl.BlockSpec((1, rows, cols), lambda b: (b, 0, 0))
    rows = sum(part.shape[0] for part in returned)
    return pl.pallas_call(
        functools.partial(finish_kernel, route_index),
        grid=(balls,),
        in_specs=[whole(slots), ball(share, width), whole(weight)]
        + [whole(part) for part in returned],
        out_specs=ball(share, width),
        out_shape=jax.ShapeDtypeStruct(layer.shape, BF16),
        scratch_shapes=[pltpu.VMEM((balls * share, 1), I32)],
        compiler_params=params(),
        cost_estimate=pl.CostEstimate(
            flops=2 * balls * share * width * (rows + width),
            bytes_accessed=8 * balls * share * width, transcendentals=0,
        ),
        name="finish",
    )(slots, layer, weight, *returned)


def side_by_side(mine, other, lower, axis):
    return jnp.where(
        lower, jnp.concatenate([mine, other], axis=axis), jnp.concatenate([other, mine], axis=axis)
    )


def double(array, axis_name, step, axis):
    count = lax.axis_size(axis_name)
    other = lax.ppermute(array, axis_name, [(i, i ^ step) for i in range(count)])
    return side_by_side(array, other, (lax.axis_index(axis_name) & step) == 0, axis)


def gather_shares(array, axis_name, axis):
    count = lax.axis_size(axis_name)
    if count & (count - 1):
        return lax.all_gather(array, axis_name, axis=axis, tiled=True)
    step = 1
    while step < count:
        array = double(array, axis_name, step, axis)
        step *= 2
    return array


def exchange(rows, wide_count):
    parts = rows.reshape((wide_count, rows.shape[0] // wide_count) + rows.shape[1:])
    parts = lax.all_to_all(parts, "wide", split_axis=0, concat_axis=0, tiled=True)
    return parts.reshape(rows.shape)


def earlier_sum(values):
    return jnp.cumsum(values, axis=-1, dtype=I32) - values


def query_step(rows):
    return min(TILE, rows)


def sorted_places(label, fill, own_blocks, labels, key_parts, tile):
    member = (label[None, :] == jnp.arange(labels, dtype=I32)[:, None]).astype(I32)
    own = member[:, :own_blocks]
    own_total = jnp.sum(own, axis=1, dtype=I32)
    own_start = earlier_sum(own_total)
    own_end = own_start + own_total
    query_at = jnp.sum(own * (own_start[:, None] + earlier_sum(own)), axis=0, dtype=I32)
    query_place = jnp.where(
        label[:own_blocks, None] >= 0,
        query_at[:, None] * BLK + jnp.arange(BLK, dtype=I32)[None, :],
        -1,
    ).reshape(-1)
    usable = member * fill[None, :]
    key_total = jnp.sum(usable, axis=1, dtype=I32)
    key_start = earlier_sum(key_total)
    key_end = key_start + key_total
    key_at = jnp.sum(member * (key_start[:, None] + earlier_sum(usable)), axis=0, dtype=I32)
    point = jnp.arange(BLK, dtype=I32)[None, :]
    key_place = jnp.where(point < fill[:, None], key_at[:, None] + point, -1).reshape(-1)
    step = query_step(own_blocks * BLK)
    tiles = own_blocks * BLK // step
    first = jnp.arange(tiles, dtype=I32)[:, None] * step
    meets = (own_start[None, :] * BLK < first + step) & (own_end[None, :] * BLK > first)
    meets = meets & (own_total[None, :] > 0)
    low = jnp.min(jnp.where(meets, key_start[None, :], label.shape[0] * BLK), axis=1)
    high = jnp.max(jnp.where(meets, key_end[None, :], 0), axis=1)
    low_tile = low // tile
    count = jnp.where(high > 0, (high + tile - 1) // tile - low_tile, 0)
    live = [jnp.broadcast_to(jnp.sum(total), count.shape) for total in (own_total * BLK, key_total)]
    limits = jnp.stack([jnp.where(high > 0, low_tile, 0), count] + live, axis=1)
    bounds = jnp.stack([own_start * BLK, own_end * BLK, key_start, key_end])
    bounds = jnp.pad(bounds, ((0, 4), (0, LANES // 2 - labels)))
    bounds = jnp.concatenate([bounds, bounds], axis=1)
    key_places = [part.reshape(1, -1) for part in jnp.split(key_place, key_parts)]
    return query_place.reshape(1, -1), query_place.reshape(-1, 1), key_places, limits, bounds


def labels_at(position, values, count):
    at = position[:, None, :] == jnp.arange(count, dtype=I32)[None, :, None]
    return jnp.sum(jnp.where(at, values[:, None, :], 0), axis=-1, dtype=I32)


def second_attention(places, own_rows, key_parts, weight, eager):
    query_row, _, _, limits, _ = places
    rows, width = own_rows.shape
    factor = math.log2(math.e) / math.sqrt(width // HEADS)
    query = arrange(limits, own_rows, query_row, weight, factor)
    return rotated_attention(
        places, query, key_parts, weight, query_step(rows), min(TILE, rows), eager
    )


def by_slots(normed, slots_of, route_index, codes, index, capacity, weight):
    wide_count = codes.shape[0]
    slots = wide_count * capacity
    packed, codes = lax.optimization_barrier((pack(slots_of, route_index, normed, slots * BLK), codes))
    arrived = exchange(packed, wide_count)
    mine = (codes // (2 * BLK)) == index
    rank = jnp.where(mine, earlier_sum(mine.astype(I32)), -1)
    found = labels_at(rank, codes % (2 * BLK) + 1, capacity).reshape(slots)
    live = found > 0
    label = jnp.where(live, (found - 1) // BLK, -1)
    fill = jnp.where(live, (found - 1) % BLK + 1, 0)
    places = sorted_places(label, fill, slots, 2, 1, min(TILE, slots * BLK))
    return [exchange(second_attention(places, arrived, [arrived], weight, 1), wide_count)]


def lower_mask(size):
    return jnp.where(iota((size, size), 0) < iota((size, size), 1), 1.0, 0.0).astype(BF16)


def ones_where(condition):
    return jnp.where(condition, 1.0, 0.0).astype(BF16)


def to_row(column):
    size = column.shape[0]
    same = iota((size, size), 0) == iota((size, size), 1)
    return jnp.sum(jnp.where(same, column, 0.0), axis=0, keepdims=True)


def route_kernel(
    wide_count, capacity, unit, here_ref, codes_ref, starts_ref, slots_ref, straddle_ref
):
    block_count = codes_ref.shape[1]
    lane = iota((1, LANES), 1)
    destination = codes_ref[...] // (2 * BLK)
    worst = jnp.zeros((1, LANES), F32)
    for side in range(2):
        part = destination[side * wide_count : (side + 1) * wide_count]
        held = jnp.zeros((wide_count, LANES), F32)
        for d in range(wide_count):
            count = jnp.sum(jnp.where(part == d, 1.0, 0.0), axis=1, keepdims=True)
            held = jnp.where(lane == d, count, held)
        load = jnp.sum(held, axis=0, keepdims=True)
        starts = jnp.zeros((wide_count, LANES), F32)
        for d in range(wide_count):
            other = load[:, d : d + 1]
            earlier = (other > load) | ((other == load) & (d < lane))
            starts = starts + jnp.where(earlier, held[:, d : d + 1], 0.0)
        starts_ref[pl.ds(side * wide_count, wide_count), :] = starts
        run = jnp.floor(starts * (1.0 / unit))
        last = jnp.floor((starts + held - 1.0) * (1.0 / unit))
        low = jnp.min(jnp.where(held > 0.0, run, 1e6), axis=0, keepdims=True)
        high = jnp.max(jnp.where(held > 0.0, last, -1.0), axis=0, keepdims=True)
        worst = jnp.maximum(worst, jnp.where((high > low) & (lane < wide_count), 1.0, 0.0))
    straddle_ref[0, 0] = jnp.max(worst).astype(I32)

    core = here_ref[0]
    index = core * wide_count + here_ref[1]
    own = codes_ref[pl.ds(index, 1), :] // (2 * BLK)
    start = starts_ref[pl.ds(index, 1), :]
    member = own == iota((wide_count, block_count), 0)
    rank = mm(ones_where(member), lower_mask(block_count))
    rank = jnp.sum(jnp.where(member, rank, 0.0), axis=0, keepdims=True)
    place = rank
    for d in range(wide_count):
        place = place + jnp.where(own == d, start[:, d : d + 1], 0.0)
    place = place.astype(I32)
    run, within = place // unit, place % unit
    half = unit // 2
    away = (within // half != core).astype(I32)
    slots_ref[0:1, :] = away * (block_count // 2) + run * half + within % half
    slots_ref[1:2, :] = own * capacity + rank.astype(I32)


def route(codes, here, wide_count, capacity, unit):
    devices, block_count = codes.shape
    full = lambda shape: pl.BlockSpec(shape, lambda _: (0, 0))
    return pl.pallas_call(
        functools.partial(route_kernel, wide_count, capacity, unit),
        grid=(1,),
        in_specs=[pl.BlockSpec(memory_space=pltpu.SMEM), whole(codes)],
        out_specs=[
            full((devices, LANES)), full((8, block_count)), pl.BlockSpec(memory_space=pltpu.SMEM),
        ],
        out_shape=[
            jax.ShapeDtypeStruct((devices, LANES), F32),
            jax.ShapeDtypeStruct((8, block_count), I32),
            jax.ShapeDtypeStruct((1, 1), I32),
        ],
        compiler_params=params(),
        name="route",
    )(here, codes)


def plan_kernel(
    unit, tile, here_ref, codes_ref, starts_ref,
    query_row_ref, query_column_ref, own_key_ref, other_key_ref, limits_ref, bounds_ref,
):
    wide_count, block_count = codes_ref.shape[0] // 2, codes_ref.shape[1]
    half = unit // 2
    blocks = wide_count * half
    core, side, base = here_ref[0], here_ref[1] % 2, here_ref[1] // 2 * unit
    mine = pl.ds(pl.multiple_of(side * wide_count, wide_count), wide_count)
    codes = codes_ref[mine, :]
    destination = codes // (2 * BLK)
    members = jnp.concatenate([ones_where(destination == d) for d in range(wide_count)], axis=0)
    rank = mm(members, lower_mask(block_count))
    starts = starts_ref[mine, :]
    position = jnp.zeros(codes.shape, F32)
    for d in range(wide_count):
        at = starts[:, d : d + 1] + rank[d * wide_count : (d + 1) * wide_count]
        position = position + jnp.where(destination == d, at, 0.0)
    position = position.astype(I32) - base
    values = codes.astype(F32)

    def labels_of(which):
        columns = []
        for source in range(wide_count):
            at = iota((half, block_count), 0) + which * half == position[source : source + 1]
            found = jnp.where(at, values[source : source + 1], 0.0)
            columns.append(jnp.sum(found, axis=1, keepdims=True))
        found = to_row(jnp.concatenate(columns, axis=0)).astype(I32)
        member = found // BLK == iota((LANES, blocks), 0) % (LANES // 2)
        return member, found % BLK + 1

    earlier = lower_mask(blocks)
    below = iota((LANES, LANES), 1) < iota((LANES, LANES), 0) % (LANES // 2)

    def begin(total):
        return jnp.sum(jnp.where(below, to_row(total), 0.0), axis=1, keepdims=True)

    def place_of(member, at):
        once = member & (iota(member.shape, 0) < LANES // 2)
        return jnp.sum(jnp.where(once, at, 0.0), axis=0, keepdims=True).astype(I32)

    own, own_fill = labels_of(core)
    other, other_fill = labels_of(1 - core)
    own_ones = ones_where(own)
    own_total = jnp.sum(jnp.where(own, 1.0, 0.0), axis=1, keepdims=True)
    own_start = begin(own_total)
    query = place_of(own, own_start + mm(own_ones, earlier))
    query_row_ref[...] = point_row(query)
    query_column_ref[...] = point_column(query)

    fills = [jnp.where(m, f.astype(F32), 0.0) for m, f in ((own, own_fill), (other, other_fill))]
    totals = [jnp.sum(f, axis=1, keepdims=True) for f in fills]
    total = totals[0] + totals[1]
    padded = jnp.floor((total + (tile - 1)) * (1.0 / tile)) * tile
    once = iota((LANES, 1), 0) < LANES // 2
    room = jnp.sum(jnp.where(once, padded, 0.0), axis=0, keepdims=True) <= 2 * blocks * BLK
    key_start = begin(jnp.where(room, padded, total))
    key_end = key_start + total
    ranks = [mm(f.astype(BF16), earlier) for f in fills]
    spread = ones_where(iota((blocks, blocks * BLK), 1) // BLK == iota((blocks, blocks * BLK), 0))
    point = iota((1, blocks * BLK), 1) % BLK
    for ref, at, fill in (
        (own_key_ref, place_of(own, key_start + ranks[0]), own_fill),
        (other_key_ref, place_of(other, key_start + totals[0] + ranks[1]), other_fill),
    ):
        digits = jnp.concatenate([at // 32, at % 32, fill] + [jnp.zeros_like(at)] * 5, axis=0)
        digits = mm(digits.astype(F32).astype(BF16), spread).astype(I32)
        ref[...] = jnp.where(point < digits[2:3], digits[:1] * 32 + digits[1:2] + point, -1)

    rows = [to_row(c) for c in (own_start * BLK, (own_start + own_total) * BLK, key_start, key_end)]
    bounds_ref[...] = jnp.concatenate(rows + [jnp.zeros_like(rows[0])] * 4, axis=0).astype(I32)
    step = query_step(blocks * BLK)
    first = (iota((8, LANES), 0) * step).astype(F32)
    meets = (rows[0] < first + step) & (rows[1] > first) & (rows[1] > rows[0])
    low = jnp.min(jnp.where(meets, rows[2], 1e6), axis=1, keepdims=True).astype(I32)
    high = jnp.max(jnp.where(meets, rows[3], 0.0), axis=1, keepdims=True).astype(I32)
    low_tile = low // tile
    count = (high + tile - 1) // tile - low_tile
    live = jnp.max(rows[3], axis=1, keepdims=True).astype(I32)
    lane = iota((8, LANES), 1)
    limits = jnp.where(lane == 0, low_tile, jnp.where(lane == 1, count, 0))
    limits = jnp.where(lane == 2, blocks * BLK, jnp.where(lane == 3, live, limits))
    limits_ref[...] = jnp.where((lane < 2) & (high <= 0), 0, limits)


def plan(here, codes, starts, unit, tile):
    wide_count = codes.shape[0] // 2
    rows = wide_count * unit // 2 * BLK
    shapes = [(1, rows), (rows, 1), (1, rows), (1, rows), (8, LANES), (8, LANES)]
    full = lambda shape: pl.BlockSpec(shape, lambda _: (0, 0))
    outs = pl.pallas_call(
        functools.partial(plan_kernel, unit, tile),
        grid=(1,),
        in_specs=[pl.BlockSpec(memory_space=pltpu.SMEM), whole(codes), whole(starts)],
        out_specs=[full(shape) for shape in shapes],
        out_shape=[jax.ShapeDtypeStruct(shape, I32) for shape in shapes],
        compiler_params=params(),
        cost_estimate=pl.CostEstimate(flops=1 << 33, bytes_accessed=1 << 22, transcendentals=0),
        name="plan",
    )(here, codes, starts)
    return outs[0], outs[1], outs[2:4], outs[4], outs[5]


def by_chips(normed, slots, here, codes, starts, weight):
    wide_count, block_count = codes.shape[0] // 2, codes.shape[1]
    unit = 2 * block_count // wide_count
    units = wide_count // 2
    rows_half = block_count * BLK // 2
    swap = lambda array: lax.ppermute(array, "narrow", [(0, 1), (1, 0)])
    is_first = lax.axis_index("narrow") == 0

    def pair_up(kept, taken):
        low = jnp.where(is_first, kept, taken).reshape(units, 1, rows_half // units, -1)
        high = jnp.where(is_first, taken, kept).reshape(units, 1, rows_half // units, -1)
        return jnp.concatenate([low, high], axis=1).reshape(2 * rows_half, -1)

    def take_apart(array):
        both = array.reshape(units, 2, rows_half // units, -1)
        low, high = both[:, 0].reshape(rows_half, -1), both[:, 1].reshape(rows_half, -1)
        return jnp.where(is_first, low, high), jnp.where(is_first, high, low)

    taken = swap(pack(slots, 0, normed, rows_half, rows_half))
    kept = pack(slots, 0, normed, rows_half)
    arrived = exchange(pair_up(kept, taken), wide_count)
    places = plan(here, codes, starts, unit, min(TILE, 2 * rows_half))
    arrived, places = lax.optimization_barrier((arrived, places))
    mixture = second_attention(places, arrived, [arrived, swap(arrived)], weight, 2)
    kept, given = take_apart(exchange(mixture, wide_count))
    return [kept, swap(given)]


def on_device(
    points, counts, destination, rotated_ball, qkv_first, out_first, qkv_second, out_second
):
    balls, share, width = points.shape
    wide_count, narrow_count = lax.axis_size("wide"), lax.axis_size("narrow")
    block_count = destination.size
    capacity = max(2, 2 * block_count // wide_count)

    flat = (block_count,)
    dest_flat = destination.reshape(flat)
    code = (dest_flat * 2 + rotated_ball.reshape(flat)) * BLK + counts.reshape(flat) - 1
    power = not wide_count & (wide_count - 1)
    paired = narrow_count == 2 and power and wide_count > 1 and 2 * wide_count <= LANES // 2
    paired = paired and block_count % wide_count == 0 and capacity * wide_count == 2 * block_count
    paired = paired and TILE <= block_count * BLK <= 8 * TILE and block_count % TILE == 0

    codes = code.reshape(1, 1, block_count)
    if paired:
        cores = [(0, 1), (1, 0)]
        chips = [(i, i ^ 1) for i in range(wide_count)]
        both = [(i, i ^ 3) for i in range(2 * wide_count)]
        mine = (codes, lax.ppermute(codes, "narrow", cores))
        theirs = (
            lax.ppermute(codes, "wide", chips), lax.ppermute(codes, ("wide", "narrow"), both)
        )
        lower = lax.axis_index("narrow") == 0
        codes = side_by_side(
            side_by_side(*mine, lower, 0), side_by_side(*theirs, lower, 0),
            (lax.axis_index("wide") & 1) == 0, 1,
        )
    elif power:
        codes = double(codes, "wide", 1, 1)
    query, kv, pooled, bias = first_projection(points, counts, qkv_first)
    if narrow_count == 2:
        coarse = [pooled, lax.ppermute(pooled, "narrow", [(0, 1), (1, 0)])]
    else:
        coarse = [gather_shares(pooled, "narrow", 1)]
    results = ()
    step = 2
    if power and step < wide_count:
        codes = double(codes, "wide", step, 1)
        step *= 2
    for ball in range(balls):
        if power:
            while step < wide_count and (step < 8 << ball or ball == balls - 1):
                coarse, codes = lax.optimization_barrier((coarse, codes))
                codes = double(codes, "wide", step, 1)
                step *= 2
        results = first_attention(ball, query, kv, coarse, bias, points, out_first, results)
    if not power:
        codes = gather_shares(codes, "wide", 1)
    layer_one, normed = results
    normed = normed.reshape(balls * share, width)

    def slot_route(codes, slots, route_index):
        index = lax.axis_index("wide")
        returned = by_slots(normed, slots, route_index, codes, index, capacity, qkv_second)
        return finish(slots, route_index, layer_one, out_second, returned)

    if not paired:
        onehot = (jnp.arange(wide_count, dtype=I32)[:, None] == dest_flat[None, :]).astype(I32)
        rank = jnp.sum(earlier_sum(onehot) * onehot, axis=0, dtype=I32)
        return slot_route(codes[0], (dest_flat * capacity + rank).reshape(1, -1), 0)

    core = lax.axis_index("narrow")
    here = jnp.stack([core, lax.axis_index("wide")]).astype(I32)
    unit = 2 * block_count // wide_count
    codes = codes.reshape(2 * wide_count, block_count)
    starts, slots, straddle = route(codes, here, wide_count, capacity, unit)
    def chip_route():
        returned = by_chips(normed, slots, here, codes, starts, qkv_second)
        return finish(slots, 0, layer_one, out_second, returned)

    def own_labels():
        return codes.reshape(2, wide_count, block_count)[core]

    return lax.cond(
        straddle[0, 0] == 0, chip_route, lambda: slot_route(own_labels(), slots, 1)
    )


def solution(mesh):
    split = P("wide", "narrow")
    in_specs = (P("wide", "narrow", None), split, split, split, P(), P(), P(), P())
    out_specs = P("wide", "narrow", None)
    return jax.shard_map(
        on_device, mesh=mesh, in_specs=in_specs, out_specs=out_specs, check_vma=False
    )
```

```python
import functools
import math

import jax
import jax.numpy as jnp
from jax import lax
from jax.experimental import pallas as pl
from jax.experimental.pallas import tpu as pltpu
from jax.sharding import PartitionSpec as P

HEADS = 8
BLK = 4
EPSILON = 1e-06
NEGATIVE = -1e30
LANES = 128
TILE = 256
VMEM_LIMIT = 56 * 1024 * 1024
BF16 = jnp.bfloat16
F32 = jnp.float32
I32 = jnp.int32

NT = (((1,), (1,)), ((), ()))


def iota(shape, axis):
    return lax.broadcasted_iota(I32, shape, axis)


def mm(left, right):
    return jnp.dot(left, right, preferred_element_type=F32)


def mm_t(left, right):
    return lax.dot_general(left, right, NT, preferred_element_type=F32)


def params():
    return pltpu.CompilerParams(vmem_limit_bytes=VMEM_LIMIT)


def whole(array):
    return pl.BlockSpec(array.shape, lambda *_: (0,) * len(array.shape))


def normalize(rows):
    return (rows * lax.rsqrt(jnp.mean(rows * rows, axis=-1, keepdims=True) + EPSILON)).astype(BF16)


def project_rows(normed, weight, width):
    factor = math.log2(math.e) / math.sqrt(width // HEADS)
    query = (mm(normed, weight[:, :width]) * factor).astype(BF16)
    return query, mm(normed, weight[:, width:]).astype(BF16)


def block_digits(values):
    digits = jnp.concatenate([values // 32, values % 32] + [jnp.zeros_like(values)] * 6, axis=0)
    return digits.astype(F32).astype(BF16)


def point_row(values):
    blocks = values.shape[1]
    spread = iota((blocks, blocks * BLK), 1) // BLK == iota((blocks, blocks * BLK), 0)
    digits = mm(block_digits(values), jnp.where(spread, 1.0, 0.0).astype(BF16)).astype(I32)
    return (digits[:1] * 32 + digits[1:2]) * BLK + iota((1, blocks * BLK), 1) % BLK


def point_column(values):
    blocks = values.shape[1]
    spread = iota((blocks * BLK, blocks), 0) // BLK == iota((blocks * BLK, blocks), 1)
    digits = mm_t(jnp.where(spread, 1.0, 0.0).astype(BF16), block_digits(values)).astype(I32)
    return (digits[:, :1] * 32 + digits[:, 1:2]) * BLK + iota((blocks * BLK, 1), 0) % BLK


def own_half(lane, head):
    return (lane < LANES // 2) if head == 0 else (lane >= LANES // 2)


def softmax_mix(scores, values):
    highest = functools.reduce(jnp.maximum, [jnp.max(s, axis=-1, keepdims=True) for s in scores])
    total = None
    for s, v in zip(scores, values):
        wide = jnp.concatenate([v, jnp.ones_like(v)], axis=1)
        part = mm(jnp.exp2(s - highest).astype(BF16), wide)
        total = part if total is None else total + part
    return total[:, :LANES] / total[:, LANES:]


def first_projection_kernel(
    width, points_ref, counts_ref, weight_ref, query_ref, kv_ref, pooled_ref, bias_ref
):
    normed = normalize(points_ref[0].astype(F32))
    query, kv = project_rows(normed, weight_ref, width)
    query_ref[0] = query
    kv_ref[0] = kv
    share = normed.shape[0]
    blocks = share // BLK
    block = iota((blocks, share), 0)
    point = iota((blocks, share), 1)
    own = point // BLK == block
    counts = jnp.broadcast_to(counts_ref[0], (8, blocks)).astype(F32).astype(BF16)
    fill = mm(counts, jnp.where(own, 1.0, 0.0).astype(BF16))[:1].astype(I32)
    usable = point[:1] % BLK < fill
    bias_ref[0] = jnp.where(usable, 0.0, NEGATIVE)
    chosen = jnp.where(own & usable, 1.0, 0.0)
    count = jnp.sum(chosen, axis=1, keepdims=True)
    pooled_ref[0] = (mm(chosen.astype(BF16), kv) / count).astype(BF16)


def first_projection(points, counts, weight):
    balls, share, width = points.shape
    blocks = share // BLK
    ball = lambda rows, cols: pl.BlockSpec((1, rows, cols), lambda b: (b, 0, 0))
    return pl.pallas_call(
        functools.partial(first_projection_kernel, width),
        grid=(balls,),
        in_specs=[ball(share, width), ball(1, blocks), whole(weight)],
        out_specs=[
            ball(share, width), ball(share, 2 * width), ball(blocks, 2 * width), ball(1, share),
        ],
        out_shape=[
            jax.ShapeDtypeStruct((balls, share, width), BF16),
            jax.ShapeDtypeStruct((balls, share, 2 * width), BF16),
            jax.ShapeDtypeStruct((balls, blocks, 2 * width), BF16),
            jax.ShapeDtypeStruct((balls, 1, share), F32),
        ],
        compiler_params=params(),
        cost_estimate=pl.CostEstimate(
            flops=2 * balls * share * width * 3 * width, bytes_accessed=8 * balls * share * width,
            transcendentals=0,
        ),
        name="first_projection",
    )(points, counts.reshape(balls, 1, blocks), weight)


def joined(parts):
    return parts[0] if len(parts) == 1 else jnp.concatenate(parts, axis=0)


def first_attention_kernel(
    width, shares, query_ref, kv_ref, bias_ref, points_ref, out_ref, *refs
):
    coarse_refs = refs[:shares]
    layer_ref, normed_ref, attended = refs[-3:]
    share = points_ref.shape[1]
    tile = min(2 * TILE, share)
    bias = bias_ref[0]

    def one_pair(pair, carry):
        at = pl.multiple_of(pair * LANES, LANES)
        value_at = pl.multiple_of(width + pair * LANES, LANES)
        keys, values = kv_ref[0, :, pl.ds(at, LANES)], kv_ref[0, :, pl.ds(value_at, LANES)]
        coarse_keys = joined([ref[0, :, pl.ds(at, LANES)] for ref in coarse_refs])
        coarse_values = joined([ref[0, :, pl.ds(value_at, LANES)] for ref in coarse_refs])
        for row in range(0, share, tile):
            query = query_ref[0, pl.ds(row, tile), pl.ds(at, LANES)]
            lane = iota(query.shape, 1)
            results = []
            for head in range(2):
                own = own_half(lane, head)
                q = jnp.where(own, query, jnp.zeros_like(query))
                results.append(
                    softmax_mix(
                        [mm_t(q, keys) + bias, mm_t(q, coarse_keys)], [values, coarse_values]
                    )
                )
            mixture = jnp.where(own_half(lane, 0), results[0], results[1])
            attended[pl.ds(row, tile), pl.ds(at, LANES)] = mixture.astype(BF16)
        return carry

    lax.fori_loop(0, width // LANES, one_pair, 0, unroll=4)
    layer = points_ref[0].astype(F32) + mm(attended[...], out_ref[...])
    layer = layer.astype(BF16)
    layer_ref[0] = layer
    normed_ref[0] = normalize(layer.astype(F32))


def first_attention(index, query, kv, coarse, bias, points, weight, earlier):
    balls, share, width = points.shape
    coarse_rows = sum(part.shape[1] for part in coarse)
    ball = lambda rows, cols: pl.BlockSpec((1, rows, cols), lambda _: (index, 0, 0))
    return pl.pallas_call(
        functools.partial(first_attention_kernel, width, len(coarse)),
        grid=(1,),
        in_specs=[
            ball(share, width), ball(share, 2 * width), ball(1, share), ball(share, width),
            whole(weight),
        ] + [ball(part.shape[1], 2 * width) for part in coarse]
        + [pl.BlockSpec(memory_space=pl.ANY)] * len(earlier),
        out_specs=[ball(share, width), ball(share, width)],
        out_shape=[jax.ShapeDtypeStruct((balls, share, width), BF16)] * 2,
        input_output_aliases={5 + len(coarse) + i: i for i in range(len(earlier))},
        scratch_shapes=[pltpu.VMEM((share, width), BF16)],
        compiler_params=params(),
        cost_estimate=pl.CostEstimate(
            flops=16 * share * (share + coarse_rows) * width,
            bytes_accessed=16 * share * width,
            transcendentals=HEADS * share * (share + coarse_rows),
        ),
        name="first_attention",
    )(query, kv, bias, points, weight, *coarse, *earlier)


def pack_kernel(route_index, offset, slots_ref, rows_ref, packed_ref):
    step = packed_ref.shape[0]
    target = offset + pl.program_id(0) * step + iota((step, rows_ref.shape[0]), 0)
    slot = point_row(slots_ref[route_index : route_index + 1, :])
    chosen = jnp.where(target == slot, 1.0, 0.0).astype(BF16)
    packed_ref[...] = mm(chosen, rows_ref[...]).astype(BF16)


def pack(slots, route_index, rows, packed_rows, offset=0):
    count, width = rows.shape
    step = min(2 * TILE, packed_rows)
    return pl.pallas_call(
        functools.partial(pack_kernel, route_index, offset),
        grid=(packed_rows // step,),
        in_specs=[whole(slots), whole(rows)],
        out_specs=pl.BlockSpec((step, width), lambda t: (t, 0)),
        out_shape=jax.ShapeDtypeStruct((packed_rows, width), BF16),
        compiler_params=params(),
        cost_estimate=pl.CostEstimate(
            flops=2 * packed_rows * width * count, bytes_accessed=4 * packed_rows * width,
            transcendentals=0,
        ),
        name="pack",
    )(slots, rows)


def pack_beside_kernel(here_ref, slots_ref, rows_ref, taken_ref, out_ref):
    units, _, rows, width = out_ref.shape
    slot = point_row(slots_ref[0:1, :])
    chosen = jnp.where(iota((units * rows, rows_ref.shape[0]), 0) == slot, 1.0, 0.0).astype(BF16)
    packed = mm(chosen, rows_ref[...]).astype(BF16)
    core = here_ref[0]
    out_ref[:, pl.ds(core, 1)] = packed.reshape(units, 1, rows, width)
    out_ref[:, pl.ds(1 - core, 1)] = taken_ref[...].reshape(units, 1, rows, width)


def pack_beside(here, slots, rows, taken, units):
    half, width = taken.shape
    shape = (units, 2, half // units, width)
    out = pl.pallas_call(
        pack_beside_kernel,
        grid=(1,),
        in_specs=[
            pl.BlockSpec(memory_space=pltpu.SMEM), whole(slots), whole(rows), whole(taken),
        ],
        out_specs=pl.BlockSpec(shape, lambda _: (0, 0, 0, 0)),
        out_shape=jax.ShapeDtypeStruct(shape, BF16),
        compiler_params=params(),
        cost_estimate=pl.CostEstimate(
            flops=2 * half * width * rows.shape[0], bytes_accessed=8 * half * width,
            transcendentals=0,
        ),
        name="pack_beside",
    )(here, slots, rows, taken)
    return out.reshape(2 * half, width)


def arrange_kernel(factor, limits_ref, rows_ref, place_ref, weight_ref, out_ref):
    tile, width = out_ref.shape
    first = pl.program_id(0) * tile

    @pl.when(first < limits_ref[0, 2])
    def _():
        target = first + iota((tile, rows_ref.shape[0]), 0)
        chosen = jnp.where(target == point_row(place_ref[...]), 1.0, 0.0).astype(BF16)
        normed = mm(chosen, rows_ref[...]).astype(BF16)
        out_ref[...] = (mm(normed, weight_ref[...]) * factor).astype(BF16)

    @pl.when(first >= limits_ref[0, 2])
    def _():
        out_ref[...] = jnp.zeros_like(out_ref)


def arrange(places, rows, weight):
    place, _, limits, _ = places
    count, width = rows.shape
    factor = math.log2(math.e) / math.sqrt(width // HEADS)
    tile = min(2 * TILE, count)
    return pl.pallas_call(
        functools.partial(arrange_kernel, factor),
        grid=(count // tile,),
        in_specs=[
            pl.BlockSpec(memory_space=pltpu.SMEM), whole(rows), whole(place),
            pl.BlockSpec((width, width), lambda t: (0, 0)),
        ],
        out_specs=pl.BlockSpec((tile, width), lambda t: (t, 0)),
        out_shape=jax.ShapeDtypeStruct((count, width), BF16),
        compiler_params=params(),
        cost_estimate=pl.CostEstimate(
            flops=2 * count * width * (count + width), bytes_accessed=4 * count * width,
            transcendentals=0,
        ),
        name="arrange",
    )(limits, rows, place, weight)


def rotated_attention_kernel(
    parts, step, tile, eager, limits_ref, bounds_ref, place_ref, query_ref, key_weight_ref,
    value_weight_ref, *refs
):
    rows_refs, key_places = refs[:parts], refs[parts : 2 * parts]
    mixture_ref, attended, marked, values_all, column = refs[2 * parts :]
    query_rows, width = query_ref.shape
    key_rows = values_all.shape[0]
    pairs = width // LANES
    portion = min(2 * tile, key_rows)

    def inside(rows, first, which):
        row = first + iota((rows, LANES), 0)
        return (row >= bounds_ref[which : which + 1, :]) & (row < bounds_ref[which + 1 : which + 2, :])

    def mark(first, keys):
        span = pl.ds(first, portion)
        closed = jnp.where(inside(portion, first, 2), 0.0, NEGATIVE).astype(BF16)
        lane = iota((portion, LANES), 1)
        for pair in range(pairs):
            at = slice(pair * LANES, (pair + 1) * LANES)
            for head in range(2):
                marked[head, span, at] = jnp.where(own_half(lane, head), keys[:, at], closed)

    def no_keys(index, carry):
        first = pl.multiple_of(index * portion, portion)
        values_all[pl.ds(first, portion), :] = jnp.zeros((portion, width), BF16)
        mark(first, jnp.zeros((portion, width), BF16))
        return carry

    def make_keys(index, carry):
        first = pl.multiple_of(index * portion, portion)
        normed = None
        for rows_ref, key_place in zip(rows_refs, key_places):
            target = first + iota((portion, key_place.shape[1]), 0)
            chosen = jnp.where(target == key_place[...], 1.0, 0.0).astype(BF16)
            part = mm(chosen, rows_ref[...])
            normed = part if normed is None else normed + part
        normed = normed.astype(BF16)
        keys = mm(normed, key_weight_ref[...]).astype(BF16)
        values_all[pl.ds(first, portion), :] = mm(normed, value_weight_ref[...]).astype(BF16)
        mark(first, keys)
        return carry

    live = (limits_ref[0, 3] + portion - 1) // portion
    lax.fori_loop(0, live, make_keys, 0)
    lax.fori_loop(live, key_rows // portion, no_keys, 0)

    def attend(index, first_key, keys, pair):
        lanes = pl.ds(pl.multiple_of(pair * LANES, LANES), LANES)
        rows = pl.ds(pl.multiple_of(index * step, step), step)
        span = pl.ds(pl.multiple_of(first_key, tile), keys)
        query = query_ref[rows, lanes]
        values = values_all[span, lanes]
        label = jnp.where(inside(step, index * step, 0), 1.0, 0.0).astype(BF16)
        lane = iota(query.shape, 1)
        results = []
        for head in range(2):
            q = jnp.where(own_half(lane, head), query, label)
            results.append(softmax_mix([mm_t(q, marked[head, span, lanes])], [values]))
        mixture = jnp.where(own_half(lane, 0), results[0], results[1])
        attended[rows, lanes] = mixture.astype(BF16)

    def one_query_tile(index, carry):
        first_tile, tiles = limits_ref[index, 0], limits_ref[index, 1]

        @pl.when(tiles == 0)
        def _():
            rows = pl.ds(pl.multiple_of(index * step, step), step)
            attended[rows, :] = jnp.zeros((step, attended.shape[1]), BF16)

        all_tiles = key_rows // tile
        fewer = 0
        for count in sorted({min(count, all_tiles) for count in (1, 2, 3, 4, 6, 8, all_tiles)}):

            @pl.when((tiles > fewer) & (tiles <= count))
            def _(count=count):
                together = math.gcd(pairs, 4 if 2 * count <= eager else 2 if count <= eager else 1)
                first_key = jnp.minimum(first_tile, all_tiles - count) * tile

                def some_pairs(step, inner):
                    for pair in range(together):
                        attend(index, first_key, count * tile, step * together + pair)
                    return inner

                lax.fori_loop(0, pairs // together, some_pairs, 0)

            fewer = count
        return carry

    lax.fori_loop(0, query_rows // step, one_query_tile, 0)

    def one_tile(index, carry):
        at = pl.multiple_of(index * step, step)
        place = column[pl.ds(at, step), :]
        chosen = jnp.where(iota((step, query_rows), 1) == place, 1.0, 0.0).astype(BF16)
        mixture_ref[pl.ds(at, step), :] = mm(chosen, attended[...]).astype(BF16)
        return carry

    column[...] = point_column(place_ref[...])
    lax.fori_loop(0, query_rows // step, one_tile, 0)


def rotated_attention(places, query, parts, weight, key_rows, eager):
    place, key_places, limits, bounds = places
    rows, width = query.shape
    step, tile = query_step(rows), min(TILE, rows)
    return pl.pallas_call(
        functools.partial(rotated_attention_kernel, len(parts), step, tile, eager),
        grid=(1,),
        in_specs=[
            pl.BlockSpec(memory_space=pltpu.SMEM), whole(bounds), whole(place), whole(query),
            pl.BlockSpec((width, width), lambda _: (0, 1)), pl.BlockSpec((width, width), lambda _: (0, 2)),
        ] + [whole(array) for array in list(parts) + list(key_places)],
        out_specs=pl.BlockSpec((rows, width), lambda _: (0, 0)),
        out_shape=jax.ShapeDtypeStruct((rows, width), BF16),
        scratch_shapes=[
            pltpu.VMEM((rows, width), BF16), pltpu.VMEM((2, key_rows, width), BF16),
            pltpu.VMEM((key_rows, width), BF16), pltpu.VMEM((rows, 1), I32),
        ],
        compiler_params=params(),
        cost_estimate=pl.CostEstimate(
            flops=8 * rows * key_rows * width, bytes_accessed=10 * rows * width,
            transcendentals=rows * key_rows * HEADS // 2,
        ),
        name="rotated_attention",
    )(limits, bounds, place, query, weight, weight, *parts, *key_places)


def finish_kernel(route_index, slots_ref, layer_ref, weight_ref, *refs):
    returned, result_ref, all_slots = refs[:-2], refs[-2], refs[-1]
    share = layer_ref.shape[1]

    @pl.when(pl.program_id(0) == 0)
    def _():
        all_slots[...] = point_column(slots_ref[route_index : route_index + 1, :])

    slot = all_slots[pl.ds(pl.multiple_of(pl.program_id(0) * share, share), share), :]
    attended, first = None, 0
    for part in returned:
        target = first + iota((share, part.shape[0]), 1)
        found = mm(jnp.where(target == slot, 1.0, 0.0).astype(BF16), part[...])
        attended = found if attended is None else attended + found
        first += part.shape[0]
    layer = layer_ref[0].astype(F32)
    result_ref[0] = (layer + mm(attended.astype(BF16), weight_ref[...])).astype(BF16)


def finish(slots, route_index, layer, weight, returned):
    balls, share, width = layer.shape
    ball = lambda rows, cols: pl.BlockSpec((1, rows, cols), lambda b: (b, 0, 0))
    rows = sum(part.shape[0] for part in returned)
    return pl.pallas_call(
        functools.partial(finish_kernel, route_index),
        grid=(balls,),
        in_specs=[whole(slots), ball(share, width), whole(weight)]
        + [whole(part) for part in returned],
        out_specs=ball(share, width),
        out_shape=jax.ShapeDtypeStruct(layer.shape, BF16),
        scratch_shapes=[pltpu.VMEM((balls * share, 1), I32)],
        compiler_params=params(),
        cost_estimate=pl.CostEstimate(
            flops=2 * balls * share * width * (rows + width),
            bytes_accessed=8 * balls * share * width, transcendentals=0,
        ),
        name="finish",
    )(slots, layer, weight, *returned)


def side_by_side(mine, other, lower, axis):
    return jnp.where(
        lower, jnp.concatenate([mine, other], axis=axis), jnp.concatenate([other, mine], axis=axis)
    )


def double(array, axis_name, step, axis):
    count = lax.axis_size(axis_name)
    other = lax.ppermute(array, axis_name, [(i, i ^ step) for i in range(count)])
    return side_by_side(array, other, (lax.axis_index(axis_name) & step) == 0, axis)


def gather_shares(array, axis_name, axis):
    count = lax.axis_size(axis_name)
    if count & (count - 1):
        return lax.all_gather(array, axis_name, axis=axis, tiled=True)
    step = 1
    while step < count:
        array = double(array, axis_name, step, axis)
        step *= 2
    return array


def exchange(rows, wide_count):
    parts = rows.reshape((wide_count, rows.shape[0] // wide_count) + rows.shape[1:])
    parts = lax.all_to_all(parts, "wide", split_axis=0, concat_axis=0, tiled=True)
    return parts.reshape(rows.shape)


def earlier_sum(values):
    return jnp.cumsum(values, axis=-1, dtype=I32) - values


def query_step(rows):
    return min(TILE, rows)


def sorted_places(label, fill, own_blocks, labels, key_parts, tile):
    member = (label[None, :] == jnp.arange(labels, dtype=I32)[:, None]).astype(I32)
    own = member[:, :own_blocks]
    own_total = jnp.sum(own, axis=1, dtype=I32)
    own_start = earlier_sum(own_total)
    own_end = own_start + own_total
    query_at = jnp.sum(own * (own_start[:, None] + earlier_sum(own)), axis=0, dtype=I32)
    nowhere = 2 * own_blocks
    query_place = jnp.where(label[:own_blocks] >= 0, query_at, nowhere).reshape(1, -1)
    usable = member * fill[None, :]
    key_total = jnp.sum(usable, axis=1, dtype=I32)
    padded = (key_total + tile - 1) // tile * tile
    room = jnp.sum(padded) <= label.shape[0] * BLK
    key_start = earlier_sum(jnp.where(room, padded, key_total))
    key_end = key_start + key_total
    key_at = jnp.sum(member * (key_start[:, None] + earlier_sum(usable)), axis=0, dtype=I32)
    point = jnp.arange(BLK, dtype=I32)[None, :]
    key_place = jnp.where(point < fill[:, None], key_at[:, None] + point, -1).reshape(-1)
    step = query_step(own_blocks * BLK)
    tiles = own_blocks * BLK // step
    first = jnp.arange(tiles, dtype=I32)[:, None] * step
    meets = (own_start[None, :] * BLK < first + step) & (own_end[None, :] * BLK > first)
    meets = meets & (own_total[None, :] > 0)
    low = jnp.min(jnp.where(meets, key_start[None, :], label.shape[0] * BLK), axis=1)
    high = jnp.max(jnp.where(meets, key_end[None, :], 0), axis=1)
    low_tile = low // tile
    count = jnp.where(high > 0, (high + tile - 1) // tile - low_tile, 0)
    live = (jnp.sum(own_total) * BLK, jnp.max(key_end))
    live = [jnp.broadcast_to(number, count.shape) for number in live]
    limits = jnp.stack([jnp.where(high > 0, low_tile, 0), count] + live, axis=1)
    bounds = jnp.stack([own_start * BLK, own_end * BLK, key_start, key_end])
    bounds = jnp.pad(bounds, ((0, 4), (0, LANES // 2 - labels)))
    bounds = jnp.concatenate([bounds, bounds], axis=1)
    key_places = [part.reshape(1, -1) for part in jnp.split(key_place, key_parts)]
    return query_place, key_places, limits, bounds


def labels_at(position, values, count):
    at = position[:, None, :] == jnp.arange(count, dtype=I32)[None, :, None]
    return jnp.sum(jnp.where(at, values[:, None, :], 0), axis=-1, dtype=I32)


def by_slots(normed, slots_of, route_index, codes, index, capacity, weight):
    wide_count = codes.shape[0]
    slots = wide_count * capacity
    packed, codes = lax.optimization_barrier((pack(slots_of, route_index, normed, slots * BLK), codes))
    arrived = exchange(packed, wide_count)
    mine = (codes // (2 * BLK)) == index
    rank = jnp.where(mine, earlier_sum(mine.astype(I32)), -1)
    found = labels_at(rank, codes % (2 * BLK) + 1, capacity).reshape(slots)
    live = found > 0
    label = jnp.where(live, (found - 1) // BLK, -1)
    fill = jnp.where(live, (found - 1) % BLK + 1, 0)
    places = sorted_places(label, fill, slots, 2, 1, min(TILE, slots * BLK))
    query = arrange(places, arrived, weight)
    mixture = rotated_attention(places, query, [arrived], weight, arrived.shape[0], 4)
    return [exchange(mixture, wide_count)]


def lower_mask(size):
    return jnp.where(iota((size, size), 0) < iota((size, size), 1), 1.0, 0.0).astype(BF16)


def ones_where(condition):
    return jnp.where(condition, 1.0, 0.0).astype(BF16)


def to_row(column):
    size = column.shape[0]
    same = iota((size, size), 0) == iota((size, size), 1)
    return jnp.sum(jnp.where(same, column, 0.0), axis=0, keepdims=True)


def route_kernel(
    wide_count, capacity, unit, here_ref, codes_ref, starts_ref, slots_ref, straddle_ref
):
    block_count = codes_ref.shape[1]
    lane = iota((1, LANES), 1)
    destination = codes_ref[...] // (2 * BLK)
    worst = jnp.zeros((1, LANES), F32)
    for side in range(2):
        part = destination[side * wide_count : (side + 1) * wide_count]
        held = jnp.zeros((wide_count, LANES), F32)
        for d in range(wide_count):
            count = jnp.sum(jnp.where(part == d, 1.0, 0.0), axis=1, keepdims=True)
            held = jnp.where(lane == d, count, held)
        load = jnp.sum(held, axis=0, keepdims=True)
        starts = jnp.zeros((wide_count, LANES), F32)
        for d in range(wide_count):
            other = load[:, d : d + 1]
            earlier = (other > load) | ((other == load) & (d < lane))
            starts = starts + jnp.where(earlier, held[:, d : d + 1], 0.0)
        starts_ref[pl.ds(side * wide_count, wide_count), :] = starts
        run = jnp.floor(starts * (1.0 / unit))
        last = jnp.floor((starts + held - 1.0) * (1.0 / unit))
        low = jnp.min(jnp.where(held > 0.0, run, 1e6), axis=0, keepdims=True)
        high = jnp.max(jnp.where(held > 0.0, last, -1.0), axis=0, keepdims=True)
        worst = jnp.maximum(worst, jnp.where((high > low) & (lane < wide_count), 1.0, 0.0))
    straddle_ref[0, 0] = jnp.max(worst).astype(I32)

    core = here_ref[0]
    index = core * wide_count + here_ref[1]
    own = codes_ref[pl.ds(index, 1), :] // (2 * BLK)
    start = starts_ref[pl.ds(index, 1), :]
    member = own == iota((wide_count, block_count), 0)
    rank = mm(ones_where(member), lower_mask(block_count))
    rank = jnp.sum(jnp.where(member, rank, 0.0), axis=0, keepdims=True)
    place = rank
    for d in range(wide_count):
        place = place + jnp.where(own == d, start[:, d : d + 1], 0.0)
    place = place.astype(I32)
    run, within = place // unit, place % unit
    half = unit // 2
    away = (within // half != core).astype(I32)
    slots_ref[0:1, :] = away * (block_count // 2) + run * half + within % half
    slots_ref[1:2, :] = own * capacity + rank.astype(I32)


def route(codes, here, wide_count, capacity, unit):
    devices, block_count = codes.shape
    full = lambda shape: pl.BlockSpec(shape, lambda _: (0, 0))
    return pl.pallas_call(
        functools.partial(route_kernel, wide_count, capacity, unit),
        grid=(1,),
        in_specs=[pl.BlockSpec(memory_space=pltpu.SMEM), whole(codes)],
        out_specs=[
            full((devices, LANES)), full((8, block_count)), pl.BlockSpec(memory_space=pltpu.SMEM),
        ],
        out_shape=[
            jax.ShapeDtypeStruct((devices, LANES), F32),
            jax.ShapeDtypeStruct((8, block_count), I32),
            jax.ShapeDtypeStruct((1, 1), I32),
        ],
        compiler_params=params(),
        name="route",
    )(here, codes)


def plan_kernel(
    unit, tile, here_ref, codes_ref, starts_ref,
    query_ref, limits_ref, bounds_ref, *key_refs
):
    wide_count, block_count = codes_ref.shape[0] // 2, codes_ref.shape[1]
    half = unit // 2
    blocks = wide_count * half
    core, side, base = here_ref[0], here_ref[1] % 2, here_ref[1] // 2 * unit
    mine = pl.ds(pl.multiple_of(side * wide_count, wide_count), wide_count)
    codes = codes_ref[mine, :]
    destination = codes // (2 * BLK)
    members = jnp.concatenate([ones_where(destination == d) for d in range(wide_count)], axis=0)
    rank = mm(members, lower_mask(block_count))
    starts = starts_ref[mine, :]
    position = jnp.zeros(codes.shape, F32)
    for d in range(wide_count):
        at = starts[:, d : d + 1] + rank[d * wide_count : (d + 1) * wide_count]
        position = position + jnp.where(destination == d, at, 0.0)
    position = position.astype(I32) - base
    values = codes.astype(F32) + 1.0

    def labels_of(which):
        columns = []
        for source in range(wide_count):
            at = iota((half, block_count), 0) + which * half == position[source : source + 1]
            found = jnp.where(at, values[source : source + 1], 0.0)
            columns.append(jnp.sum(found, axis=1, keepdims=True))
        found = to_row(jnp.concatenate(columns, axis=0)).astype(I32) + (BLK - 1)
        member = found // BLK - 1 == iota((LANES, blocks), 0) % (LANES // 2)
        return member, jnp.where(member, (found % BLK + 1).astype(F32), 0.0)

    earlier = lower_mask(blocks)
    below = iota((LANES, LANES), 1) < iota((LANES, LANES), 0) % (LANES // 2)

    def begin(total):
        return jnp.sum(jnp.where(below, to_row(total), 0.0), axis=1, keepdims=True)

    def place_of(member, at):
        once = member & (iota(member.shape, 0) < LANES // 2)
        return jnp.sum(jnp.where(once, at, 0.0), axis=0, keepdims=True).astype(I32)

    parts = [labels_of(which) for which in (core, 1 - core)]
    own = parts[0][0]
    own_ones = ones_where(own)
    own_total = jnp.sum(jnp.where(own, 1.0, 0.0), axis=1, keepdims=True)
    own_start = begin(own_total)
    query = place_of(own, own_start + mm(own_ones, earlier))
    query_ref[...] = query

    totals = [jnp.sum(fill, axis=1, keepdims=True) for _, fill in parts]
    total = sum(totals)
    padded = jnp.floor((total + (tile - 1)) * (1.0 / tile)) * tile
    once = iota((LANES, 1), 0) < LANES // 2
    room = jnp.sum(jnp.where(once, padded, 0.0), axis=0, keepdims=True) <= 2 * blocks * BLK
    key_start = begin(jnp.where(room, padded, total))
    key_end = key_start + total
    spread = ones_where(iota((blocks, blocks * BLK), 1) // BLK == iota((blocks, blocks * BLK), 0))
    point = iota((1, blocks * BLK), 1) % BLK
    begins = key_start
    for ref, (member, fill), part_total in zip(key_refs, parts, totals):
        at = place_of(member, begins + mm(fill.astype(BF16), earlier))
        count = place_of(member, fill)
        digits = jnp.concatenate([at // 32, at % 32, count] + [jnp.zeros_like(at)] * 5, axis=0)
        digits = mm(digits.astype(F32).astype(BF16), spread).astype(I32)
        ref[...] = jnp.where(point < digits[2:3], digits[:1] * 32 + digits[1:2] + point, -1)
        begins = begins + part_total

    rows = [to_row(c) for c in (own_start * BLK, (own_start + own_total) * BLK, key_start, key_end)]
    bounds_ref[...] = jnp.concatenate(rows + [jnp.zeros_like(rows[0])] * 4, axis=0).astype(I32)
    step = query_step(blocks * BLK)
    first = (iota((8, LANES), 0) * step).astype(F32)
    meets = (rows[0] < first + step) & (rows[1] > first) & (rows[1] > rows[0])
    low = jnp.min(jnp.where(meets, rows[2], 1e6), axis=1, keepdims=True).astype(I32)
    high = jnp.max(jnp.where(meets, rows[3], 0.0), axis=1, keepdims=True).astype(I32)
    low_tile = low // tile
    count = (high + tile - 1) // tile - low_tile
    live = jnp.max(rows[3], axis=1, keepdims=True).astype(I32)
    lane = iota((8, LANES), 1)
    limits = jnp.where(lane == 0, low_tile, jnp.where(lane == 1, count, 0))
    limits = jnp.where(lane == 2, blocks * BLK, jnp.where(lane == 3, live, limits))
    limits_ref[...] = jnp.where((lane < 2) & (high <= 0), 0, limits)


def plan(here, codes, starts, unit, tile):
    wide_count = codes.shape[0] // 2
    rows = wide_count * unit // 2 * BLK
    shapes = [(1, rows // BLK), (8, LANES), (8, LANES)] + [(1, rows)] * 2
    full = lambda shape: pl.BlockSpec(shape, lambda _: (0, 0))
    outs = pl.pallas_call(
        functools.partial(plan_kernel, unit, tile),
        grid=(1,),
        in_specs=[pl.BlockSpec(memory_space=pltpu.SMEM), whole(codes), whole(starts)],
        out_specs=[full(shape) for shape in shapes],
        out_shape=[jax.ShapeDtypeStruct(shape, I32) for shape in shapes],
        compiler_params=params(),
        cost_estimate=pl.CostEstimate(flops=1 << 33, bytes_accessed=1 << 22, transcendentals=0),
        name="plan",
    )(here, codes, starts)
    return outs[0], outs[3:], outs[1], outs[2]


def by_chips(normed, slots, here, codes, starts, weight):
    wide_count, block_count = codes.shape[0] // 2, codes.shape[1]
    unit = 2 * block_count // wide_count
    units = wide_count // 2
    rows_half = block_count * BLK // 2
    swap = lambda array: lax.ppermute(array, "narrow", [(0, 1), (1, 0)])
    is_first = lax.axis_index("narrow") == 0

    def take_apart(array):
        both = array.reshape(units, 2, rows_half // units, -1)
        low, high = both[:, 0].reshape(rows_half, -1), both[:, 1].reshape(rows_half, -1)
        return jnp.where(is_first, low, high), jnp.where(is_first, high, low)

    taken = swap(pack(slots, 0, normed, rows_half, rows_half))
    arrived = exchange(pack_beside(here, slots, normed, taken, units), wide_count)
    tile = min(TILE, 2 * rows_half)
    places = plan(here, codes, starts, unit, tile)
    arrived, places = lax.optimization_barrier((arrived, places))
    partner = swap(arrived)
    query = arrange(places, arrived, weight)
    key_rows = 4 * rows_half

    mixture = rotated_attention(places, query, [arrived, partner], weight, key_rows, 6)
    kept, given = take_apart(exchange(mixture, wide_count))
    return [kept, swap(given)]


def on_device(
    points, counts, destination, rotated_ball, qkv_first, out_first, qkv_second, out_second
):
    balls, share, width = points.shape
    wide_count, narrow_count = lax.axis_size("wide"), lax.axis_size("narrow")
    block_count = destination.size
    capacity = max(2, 2 * block_count // wide_count)

    flat = (block_count,)
    dest_flat = destination.reshape(flat)
    code = (dest_flat * 2 + rotated_ball.reshape(flat)) * BLK + counts.reshape(flat) - 1
    power = not wide_count & (wide_count - 1)
    paired = narrow_count == 2 and power and wide_count > 1 and 2 * wide_count <= LANES // 2
    paired = paired and block_count % wide_count == 0 and capacity * wide_count == 2 * block_count
    paired = paired and TILE <= block_count * BLK <= 8 * TILE and block_count % TILE == 0

    codes = code.reshape(1, 1, block_count)
    if paired:
        cores = [(0, 1), (1, 0)]
        chips = [(i, i ^ 1) for i in range(wide_count)]
        both = [(i, i ^ 3) for i in range(2 * wide_count)]
        mine = (codes, lax.ppermute(codes, "narrow", cores))
        theirs = (
            lax.ppermute(codes, "wide", chips), lax.ppermute(codes, ("wide", "narrow"), both)
        )
        lower = lax.axis_index("narrow") == 0
        codes = side_by_side(
            side_by_side(*mine, lower, 0), side_by_side(*theirs, lower, 0),
            (lax.axis_index("wide") & 1) == 0, 1,
        )
    elif power:
        codes = double(codes, "wide", 1, 1)
    query, kv, pooled, bias = first_projection(points, counts, qkv_first)
    if narrow_count == 2:
        coarse = [pooled, lax.ppermute(pooled, "narrow", [(0, 1), (1, 0)])]
    else:
        coarse = [gather_shares(pooled, "narrow", 1)]
    results = ()
    step = 2
    if power and step < wide_count:
        codes = double(codes, "wide", step, 1)
        step *= 2
    for ball in range(balls):
        if power:
            while step < wide_count and (step < 8 << ball or ball == balls - 1):
                coarse, codes = lax.optimization_barrier((coarse, codes))
                codes = double(codes, "wide", step, 1)
                step *= 2
        results = first_attention(ball, query, kv, coarse, bias, points, out_first, results)
    if not power:
        codes = gather_shares(codes, "wide", 1)
    layer_one, normed = results
    normed = normed.reshape(balls * share, width)

    def slot_route(codes, slots, route_index):
        index = lax.axis_index("wide")
        returned = by_slots(normed, slots, route_index, codes, index, capacity, qkv_second)
        return finish(slots, route_index, layer_one, out_second, returned)

    if not paired:
        onehot = (jnp.arange(wide_count, dtype=I32)[:, None] == dest_flat[None, :]).astype(I32)
        rank = jnp.sum(earlier_sum(onehot) * onehot, axis=0, dtype=I32)
        return slot_route(codes[0], (dest_flat * capacity + rank).reshape(1, -1), 0)

    core = lax.axis_index("narrow")
    here = jnp.stack([core, lax.axis_index("wide")]).astype(I32)
    unit = 2 * block_count // wide_count
    codes = codes.reshape(2 * wide_count, block_count)
    starts, slots, straddle = route(codes, here, wide_count, capacity, unit)
    def chip_route():
        returned = by_chips(normed, slots, here, codes, starts, qkv_second)
        return finish(slots, 0, layer_one, out_second, returned)

    def own_labels():
        return codes.reshape(2, wide_count, block_count)[core]

    return lax.cond(
        straddle[0, 0] == 0, chip_route, lambda: slot_route(own_labels(), slots, 1)
    )


def solution(mesh):
    split = P("wide", "narrow")
    in_specs = (P("wide", "narrow", None), split, split, split, P(), P(), P(), P())
    out_specs = P("wide", "narrow", None)
    return jax.shard_map(
        on_device, mesh=mesh, in_specs=in_specs, out_specs=out_specs, check_vma=False
    )
```

```python
import functools
import math

import jax
import jax.numpy as jnp
from jax import lax
from jax.experimental import pallas as pl
from jax.experimental.pallas import tpu as pltpu
from jax.sharding import PartitionSpec as P

HEADS = 8
BLK = 4
EPSILON = 1e-06
NEGATIVE = -1e30
LANES = 128
TILE = 256
VMEM_LIMIT = 56 * 1024 * 1024
BF16 = jnp.bfloat16
F32 = jnp.float32
I32 = jnp.int32

NT = (((1,), (1,)), ((), ()))


def iota(shape, axis):
    return lax.broadcasted_iota(I32, shape, axis)


def mm(left, right):
    return jnp.dot(left, right, preferred_element_type=F32)


def mm_t(left, right):
    return lax.dot_general(left, right, NT, preferred_element_type=F32)


def params():
    return pltpu.CompilerParams(vmem_limit_bytes=VMEM_LIMIT)


def whole(array):
    return pl.BlockSpec(array.shape, lambda *_: (0,) * len(array.shape))


def normalize(rows):
    return (rows * lax.rsqrt(jnp.mean(rows * rows, axis=-1, keepdims=True) + EPSILON)).astype(BF16)


def project_rows(normed, weight, width):
    factor = math.log2(math.e) / math.sqrt(width // HEADS)
    query = (mm(normed, weight[:, :width]) * factor).astype(BF16)
    return query, mm(normed, weight[:, width:]).astype(BF16)


def block_digits(values):
    digits = jnp.concatenate([values // 32, values % 32] + [jnp.zeros_like(values)] * 6, axis=0)
    return digits.astype(F32).astype(BF16)


def point_row(values):
    blocks = values.shape[1]
    spread = iota((blocks, blocks * BLK), 1) // BLK == iota((blocks, blocks * BLK), 0)
    digits = mm(block_digits(values), jnp.where(spread, 1.0, 0.0).astype(BF16)).astype(I32)
    return (digits[:1] * 32 + digits[1:2]) * BLK + iota((1, blocks * BLK), 1) % BLK


def point_column(values):
    blocks = values.shape[1]
    spread = iota((blocks * BLK, blocks), 0) // BLK == iota((blocks * BLK, blocks), 1)
    digits = mm_t(jnp.where(spread, 1.0, 0.0).astype(BF16), block_digits(values)).astype(I32)
    return (digits[:, :1] * 32 + digits[:, 1:2]) * BLK + iota((blocks * BLK, 1), 0) % BLK


def own_half(lane, head):
    return (lane < LANES // 2) if head == 0 else (lane >= LANES // 2)


def softmax_mix(scores, values):
    highest = functools.reduce(jnp.maximum, [jnp.max(s, axis=-1, keepdims=True) for s in scores])
    total = None
    for s, v in zip(scores, values):
        wide = jnp.concatenate([v, jnp.ones_like(v)], axis=1)
        part = mm(jnp.exp2(s - highest).astype(BF16), wide)
        total = part if total is None else total + part
    return total[:, :LANES] / total[:, LANES:]


def first_projection_kernel(
    width, points_ref, counts_ref, weight_ref, query_ref, kv_ref, pooled_ref, bias_ref
):
    normed = normalize(points_ref[0].astype(F32))
    query, kv = project_rows(normed, weight_ref, width)
    query_ref[0] = query
    kv_ref[0] = kv
    share = normed.shape[0]
    blocks = share // BLK
    block = iota((blocks, share), 0)
    point = iota((blocks, share), 1)
    own = point // BLK == block
    counts = jnp.broadcast_to(counts_ref[0], (8, blocks)).astype(F32).astype(BF16)
    fill = mm(counts, jnp.where(own, 1.0, 0.0).astype(BF16))[:1].astype(I32)
    usable = point[:1] % BLK < fill
    bias_ref[0] = jnp.where(usable, 0.0, NEGATIVE)
    chosen = jnp.where(own & usable, 1.0, 0.0)
    count = jnp.sum(chosen, axis=1, keepdims=True)
    pooled_ref[0] = (mm(chosen.astype(BF16), kv) / count).astype(BF16)


def first_projection(points, counts, weight):
    balls, share, width = points.shape
    blocks = share // BLK
    ball = lambda rows, cols: pl.BlockSpec((1, rows, cols), lambda b: (b, 0, 0))
    return pl.pallas_call(
        functools.partial(first_projection_kernel, width),
        grid=(balls,),
        in_specs=[ball(share, width), ball(1, blocks), whole(weight)],
        out_specs=[
            ball(share, width), ball(share, 2 * width), ball(blocks, 2 * width), ball(1, share),
        ],
        out_shape=[
            jax.ShapeDtypeStruct((balls, share, width), BF16),
            jax.ShapeDtypeStruct((balls, share, 2 * width), BF16),
            jax.ShapeDtypeStruct((balls, blocks, 2 * width), BF16),
            jax.ShapeDtypeStruct((balls, 1, share), F32),
        ],
        compiler_params=params(),
        cost_estimate=pl.CostEstimate(
            flops=2 * balls * share * width * 3 * width, bytes_accessed=8 * balls * share * width,
            transcendentals=0,
        ),
        name="first_projection",
    )(points, counts.reshape(balls, 1, blocks), weight)


def joined(parts):
    return parts[0] if len(parts) == 1 else jnp.concatenate(parts, axis=0)


def first_attention_kernel(
    width, shares, query_ref, kv_ref, bias_ref, points_ref, out_ref, *refs
):
    coarse_refs = refs[:shares]
    layer_ref, normed_ref, attended = refs[-3:]
    share = points_ref.shape[1]
    tile = min(2 * TILE, share)
    bias = bias_ref[0]

    def one_pair(pair, carry):
        at = pl.multiple_of(pair * LANES, LANES)
        value_at = pl.multiple_of(width + pair * LANES, LANES)
        keys, values = kv_ref[0, :, pl.ds(at, LANES)], kv_ref[0, :, pl.ds(value_at, LANES)]
        coarse_keys = joined([ref[0, :, pl.ds(at, LANES)] for ref in coarse_refs])
        coarse_values = joined([ref[0, :, pl.ds(value_at, LANES)] for ref in coarse_refs])
        for row in range(0, share, tile):
            query = query_ref[0, pl.ds(row, tile), pl.ds(at, LANES)]
            lane = iota(query.shape, 1)
            results = []
            for head in range(2):
                own = own_half(lane, head)
                q = jnp.where(own, query, jnp.zeros_like(query))
                results.append(
                    softmax_mix(
                        [mm_t(q, keys) + bias, mm_t(q, coarse_keys)], [values, coarse_values]
                    )
                )
            mixture = jnp.where(own_half(lane, 0), results[0], results[1])
            attended[pl.ds(row, tile), pl.ds(at, LANES)] = mixture.astype(BF16)
        return carry

    lax.fori_loop(0, width // LANES, one_pair, 0, unroll=4)
    layer = points_ref[0].astype(F32) + mm(attended[...], out_ref[...])
    layer = layer.astype(BF16)
    layer_ref[0] = layer
    normed_ref[0] = normalize(layer.astype(F32))


def first_attention(index, query, kv, coarse, bias, points, weight, earlier):
    balls, share, width = points.shape
    coarse_rows = sum(part.shape[1] for part in coarse)
    ball = lambda rows, cols: pl.BlockSpec((1, rows, cols), lambda _: (index, 0, 0))
    return pl.pallas_call(
        functools.partial(first_attention_kernel, width, len(coarse)),
        grid=(1,),
        in_specs=[
            ball(share, width), ball(share, 2 * width), ball(1, share), ball(share, width),
            whole(weight),
        ] + [ball(part.shape[1], 2 * width) for part in coarse]
        + [pl.BlockSpec(memory_space=pl.ANY)] * len(earlier),
        out_specs=[ball(share, width), ball(share, width)],
        out_shape=[jax.ShapeDtypeStruct((balls, share, width), BF16)] * 2,
        input_output_aliases={5 + len(coarse) + i: i for i in range(len(earlier))},
        scratch_shapes=[pltpu.VMEM((share, width), BF16)],
        compiler_params=params(),
        cost_estimate=pl.CostEstimate(
            flops=16 * share * (share + coarse_rows) * width,
            bytes_accessed=16 * share * width,
            transcendentals=HEADS * share * (share + coarse_rows),
        ),
        name="first_attention",
    )(query, kv, bias, points, weight, *coarse, *earlier)


def pack_kernel(route_index, offset, slots_ref, rows_ref, packed_ref):
    step = packed_ref.shape[0]
    target = offset + pl.program_id(0) * step + iota((step, rows_ref.shape[0]), 0)
    slot = point_row(slots_ref[route_index : route_index + 1, :])
    chosen = jnp.where(target == slot, 1.0, 0.0).astype(BF16)
    packed_ref[...] = mm(chosen, rows_ref[...]).astype(BF16)


def pack(slots, route_index, rows, packed_rows, offset=0):
    count, width = rows.shape
    step = min(2 * TILE, packed_rows)
    return pl.pallas_call(
        functools.partial(pack_kernel, route_index, offset),
        grid=(packed_rows // step,),
        in_specs=[whole(slots), whole(rows)],
        out_specs=pl.BlockSpec((step, width), lambda t: (t, 0)),
        out_shape=jax.ShapeDtypeStruct((packed_rows, width), BF16),
        compiler_params=params(),
        cost_estimate=pl.CostEstimate(
            flops=2 * packed_rows * width * count, bytes_accessed=4 * packed_rows * width,
            transcendentals=0,
        ),
        name="pack",
    )(slots, rows)


def pack_beside_kernel(here_ref, slots_ref, rows_ref, taken_ref, out_ref):
    units, _, rows, width = out_ref.shape
    slot = point_row(slots_ref[0:1, :])
    chosen = jnp.where(iota((units * rows, rows_ref.shape[0]), 0) == slot, 1.0, 0.0).astype(BF16)
    packed = mm(chosen, rows_ref[...]).astype(BF16)
    core = here_ref[0]
    out_ref[:, pl.ds(core, 1)] = packed.reshape(units, 1, rows, width)
    out_ref[:, pl.ds(1 - core, 1)] = taken_ref[...].reshape(units, 1, rows, width)


def pack_beside(here, slots, rows, taken, units):
    half, width = taken.shape
    shape = (units, 2, half // units, width)
    out = pl.pallas_call(
        pack_beside_kernel,
        grid=(1,),
        in_specs=[
            pl.BlockSpec(memory_space=pltpu.SMEM), whole(slots), whole(rows), whole(taken),
        ],
        out_specs=pl.BlockSpec(shape, lambda _: (0, 0, 0, 0)),
        out_shape=jax.ShapeDtypeStruct(shape, BF16),
        compiler_params=params(),
        cost_estimate=pl.CostEstimate(
            flops=2 * half * width * rows.shape[0], bytes_accessed=8 * half * width,
            transcendentals=0,
        ),
        name="pack_beside",
    )(here, slots, rows, taken)
    return out.reshape(2 * half, width)


def arrange_kernel(factor, limits_ref, rows_ref, place_ref, weight_ref, out_ref):
    tile, width = out_ref.shape
    first = pl.program_id(0) * tile

    @pl.when(first < limits_ref[0, 2])
    def _():
        target = first + iota((tile, rows_ref.shape[0]), 0)
        chosen = jnp.where(target == point_row(place_ref[...]), 1.0, 0.0).astype(BF16)
        normed = mm(chosen, rows_ref[...]).astype(BF16)
        out_ref[...] = (mm(normed, weight_ref[...]) * factor).astype(BF16)

    @pl.when(first >= limits_ref[0, 2])
    def _():
        out_ref[...] = jnp.zeros_like(out_ref)


def arrange(places, rows, weight):
    place, _, limits, _ = places
    count, width = rows.shape
    factor = math.log2(math.e) / math.sqrt(width // HEADS)
    tile = min(2 * TILE, count)
    return pl.pallas_call(
        functools.partial(arrange_kernel, factor),
        grid=(count // tile,),
        in_specs=[
            pl.BlockSpec(memory_space=pltpu.SMEM), whole(rows), whole(place),
            pl.BlockSpec((width, width), lambda t: (0, 0)),
        ],
        out_specs=pl.BlockSpec((tile, width), lambda t: (t, 0)),
        out_shape=jax.ShapeDtypeStruct((count, width), BF16),
        compiler_params=params(),
        cost_estimate=pl.CostEstimate(
            flops=2 * count * width * (count + width), bytes_accessed=4 * count * width,
            transcendentals=0,
        ),
        name="arrange",
    )(limits, rows, place, weight)


def rotated_attention_kernel(
    parts, step, tile, eager, limits_ref, bounds_ref, place_ref, query_ref, key_weight_ref,
    value_weight_ref, *refs
):
    rows_refs, key_places = refs[:parts], refs[parts : 2 * parts]
    mixture_ref, attended, marked, values_all, column = refs[2 * parts :]
    query_rows, width = query_ref.shape
    key_rows = values_all.shape[0]
    pairs = width // LANES
    portion = min(2 * tile, key_rows)

    def inside(rows, first, which):
        row = first + iota((rows, LANES), 0)
        return (row >= bounds_ref[which : which + 1, :]) & (row < bounds_ref[which + 1 : which + 2, :])

    def mark(first, keys):
        span = pl.ds(first, portion)
        closed = jnp.where(inside(portion, first, 2), 0.0, NEGATIVE).astype(BF16)
        lane = iota((portion, LANES), 1)
        for pair in range(pairs):
            at = slice(pair * LANES, (pair + 1) * LANES)
            for head in range(2):
                marked[head, span, at] = jnp.where(own_half(lane, head), keys[:, at], closed)

    def no_keys(index, carry):
        first = pl.multiple_of(index * portion, portion)
        values_all[pl.ds(first, portion), :] = jnp.zeros((portion, width), BF16)
        mark(first, jnp.zeros((portion, width), BF16))
        return carry

    def make_keys(index, carry):
        first = pl.multiple_of(index * portion, portion)
        normed = None
        for rows_ref, key_place in zip(rows_refs, key_places):
            target = first + iota((portion, key_place.shape[1]), 0)
            chosen = jnp.where(target == key_place[...], 1.0, 0.0).astype(BF16)
            part = mm(chosen, rows_ref[...])
            normed = part if normed is None else normed + part
        normed = normed.astype(BF16)
        keys = mm(normed, key_weight_ref[...]).astype(BF16)
        values_all[pl.ds(first, portion), :] = mm(normed, value_weight_ref[...]).astype(BF16)
        mark(first, keys)
        return carry

    live = (limits_ref[0, 3] + portion - 1) // portion
    lax.fori_loop(0, live, make_keys, 0)
    lax.fori_loop(live, key_rows // portion, no_keys, 0)

    def attend(index, first_key, keys, pair):
        lanes = pl.ds(pl.multiple_of(pair * LANES, LANES), LANES)
        rows = pl.ds(pl.multiple_of(index * step, step), step)
        span = pl.ds(pl.multiple_of(first_key, tile), keys)
        query = query_ref[rows, lanes]
        values = values_all[span, lanes]
        label = jnp.where(inside(step, index * step, 0), 1.0, 0.0).astype(BF16)
        lane = iota(query.shape, 1)
        results = []
        for head in range(2):
            q = jnp.where(own_half(lane, head), query, label)
            results.append(softmax_mix([mm_t(q, marked[head, span, lanes])], [values]))
        mixture = jnp.where(own_half(lane, 0), results[0], results[1])
        attended[rows, lanes] = mixture.astype(BF16)

    def one_query_tile(index, carry):
        first_tile, tiles = limits_ref[index, 0], limits_ref[index, 1]

        @pl.when(tiles == 0)
        def _():
            rows = pl.ds(pl.multiple_of(index * step, step), step)
            attended[rows, :] = jnp.zeros((step, attended.shape[1]), BF16)

        all_tiles = key_rows // tile
        fewer = 0
        for count in sorted({min(count, all_tiles) for count in (1, 2, 3, 4, 6, 8, all_tiles)}):

            @pl.when((tiles > fewer) & (tiles <= count))
            def _(count=count):
                together = math.gcd(pairs, 4 if 2 * count <= eager else 2 if count <= eager else 1)
                first_key = jnp.minimum(first_tile, all_tiles - count) * tile

                def some_pairs(step, inner):
                    for pair in range(together):
                        attend(index, first_key, count * tile, step * together + pair)
                    return inner

                lax.fori_loop(0, pairs // together, some_pairs, 0)

            fewer = count
        return carry

    lax.fori_loop(0, query_rows // step, one_query_tile, 0)

    def one_tile(index, carry):
        at = pl.multiple_of(index * step, step)
        place = column[pl.ds(at, step), :]
        chosen = jnp.where(iota((step, query_rows), 1) == place, 1.0, 0.0).astype(BF16)
        mixture_ref[pl.ds(at, step), :] = mm(chosen, attended[...]).astype(BF16)
        return carry

    column[...] = point_column(place_ref[...])
    lax.fori_loop(0, query_rows // step, one_tile, 0)


def rotated_attention(places, query, parts, weight, key_rows, eager):
    place, key_places, limits, bounds = places
    rows, width = query.shape
    step, tile = query_step(rows), min(TILE, rows)
    return pl.pallas_call(
        functools.partial(rotated_attention_kernel, len(parts), step, tile, eager),
        grid=(1,),
        in_specs=[
            pl.BlockSpec(memory_space=pltpu.SMEM), whole(bounds), whole(place), whole(query),
            pl.BlockSpec((width, width), lambda _: (0, 1)), pl.BlockSpec((width, width), lambda _: (0, 2)),
        ] + [whole(array) for array in list(parts) + list(key_places)],
        out_specs=pl.BlockSpec((rows, width), lambda _: (0, 0)),
        out_shape=jax.ShapeDtypeStruct((rows, width), BF16),
        scratch_shapes=[
            pltpu.VMEM((rows, width), BF16), pltpu.VMEM((2, key_rows, width), BF16),
            pltpu.VMEM((key_rows, width), BF16), pltpu.VMEM((rows, 1), I32),
        ],
        compiler_params=params(),
        cost_estimate=pl.CostEstimate(
            flops=8 * rows * key_rows * width, bytes_accessed=10 * rows * width,
            transcendentals=rows * key_rows * HEADS // 2,
        ),
        name="rotated_attention",
    )(limits, bounds, place, query, weight, weight, *parts, *key_places)


def finish_kernel(route_index, here_ref, slots_ref, layer_ref, weight_ref, *refs):
    returned, result_ref, all_slots = refs[:-2], refs[-2], refs[-1]
    share = layer_ref.shape[1]

    @pl.when(pl.program_id(0) == 0)
    def _():
        all_slots[...] = point_column(slots_ref[route_index : route_index + 1, :])

    slot = all_slots[pl.ds(pl.multiple_of(pl.program_id(0) * share, share), share), :]
    attended, first = None, 0
    for part in returned:
        rows = part[...].reshape(-1, part.shape[-1])
        target = first + iota((share, rows.shape[0]), 1)
        found = mm(jnp.where(target == slot, 1.0, 0.0).astype(BF16), rows)
        attended = found if attended is None else attended + found
        first += rows.shape[0]
    layer = layer_ref[0].astype(F32)
    result_ref[0] = (layer + mm(attended.astype(BF16), weight_ref[...])).astype(BF16)


def finish(here, slots, route_index, layer, weight, returned):
    balls, share, width = layer.shape
    full = lambda shape: pl.BlockSpec(shape, lambda b, here: (0,) * len(shape))
    ball = pl.BlockSpec((1, share, width), lambda b, here: (b, 0, 0))

    def of_core(shape):
        return pl.BlockSpec((shape[0], 1) + shape[2:], lambda b, here: (0, here[0], 0, 0))

    rows = sum(part.size // width // (2 if part.ndim == 4 else 1) for part in returned)
    return pl.pallas_call(
        functools.partial(finish_kernel, route_index),
        grid_spec=pltpu.PrefetchScalarGridSpec(
            num_scalar_prefetch=1,
            grid=(balls,),
            in_specs=[full(slots.shape), ball, full(weight.shape)]
            + [of_core(part.shape) if part.ndim == 4 else full(part.shape) for part in returned],
            out_specs=ball,
            scratch_shapes=[pltpu.VMEM((balls * share, 1), I32)],
        ),
        out_shape=jax.ShapeDtypeStruct(layer.shape, BF16),
        compiler_params=params(),
        cost_estimate=pl.CostEstimate(
            flops=2 * balls * share * width * (rows + width),
            bytes_accessed=8 * balls * share * width, transcendentals=0,
        ),
        name="finish",
    )(here, slots, layer, weight, *returned)


def side_by_side(mine, other, lower, axis):
    return jnp.where(
        lower, jnp.concatenate([mine, other], axis=axis), jnp.concatenate([other, mine], axis=axis)
    )


def double(array, axis_name, step, axis):
    count = lax.axis_size(axis_name)
    other = lax.ppermute(array, axis_name, [(i, i ^ step) for i in range(count)])
    return side_by_side(array, other, (lax.axis_index(axis_name) & step) == 0, axis)


def gather_shares(array, axis_name, axis):
    count = lax.axis_size(axis_name)
    if count & (count - 1):
        return lax.all_gather(array, axis_name, axis=axis, tiled=True)
    step = 1
    while step < count:
        array = double(array, axis_name, step, axis)
        step *= 2
    return array


def exchange(rows, wide_count):
    parts = rows.reshape((wide_count, rows.shape[0] // wide_count) + rows.shape[1:])
    parts = lax.all_to_all(parts, "wide", split_axis=0, concat_axis=0, tiled=True)
    return parts.reshape(rows.shape)


def earlier_sum(values):
    return jnp.cumsum(values, axis=-1, dtype=I32) - values


def query_step(rows):
    return min(TILE, rows)


def sorted_places(label, fill, own_blocks, labels, key_parts, tile):
    member = (label[None, :] == jnp.arange(labels, dtype=I32)[:, None]).astype(I32)
    own = member[:, :own_blocks]
    own_total = jnp.sum(own, axis=1, dtype=I32)
    own_start = earlier_sum(own_total)
    own_end = own_start + own_total
    query_at = jnp.sum(own * (own_start[:, None] + earlier_sum(own)), axis=0, dtype=I32)
    nowhere = 2 * own_blocks
    query_place = jnp.where(label[:own_blocks] >= 0, query_at, nowhere).reshape(1, -1)
    usable = member * fill[None, :]
    key_total = jnp.sum(usable, axis=1, dtype=I32)
    padded = (key_total + tile - 1) // tile * tile
    room = jnp.sum(padded) <= label.shape[0] * BLK
    key_start = earlier_sum(jnp.where(room, padded, key_total))
    key_end = key_start + key_total
    key_at = jnp.sum(member * (key_start[:, None] + earlier_sum(usable)), axis=0, dtype=I32)
    point = jnp.arange(BLK, dtype=I32)[None, :]
    key_place = jnp.where(point < fill[:, None], key_at[:, None] + point, -1).reshape(-1)
    step = query_step(own_blocks * BLK)
    tiles = own_blocks * BLK // step
    first = jnp.arange(tiles, dtype=I32)[:, None] * step
    meets = (own_start[None, :] * BLK < first + step) & (own_end[None, :] * BLK > first)
    meets = meets & (own_total[None, :] > 0)
    low = jnp.min(jnp.where(meets, key_start[None, :], label.shape[0] * BLK), axis=1)
    high = jnp.max(jnp.where(meets, key_end[None, :], 0), axis=1)
    low_tile = low // tile
    count = jnp.where(high > 0, (high + tile - 1) // tile - low_tile, 0)
    live = (jnp.sum(own_total) * BLK, jnp.max(key_end))
    live = [jnp.broadcast_to(number, count.shape) for number in live]
    limits = jnp.stack([jnp.where(high > 0, low_tile, 0), count] + live, axis=1)
    bounds = jnp.stack([own_start * BLK, own_end * BLK, key_start, key_end])
    bounds = jnp.pad(bounds, ((0, 4), (0, LANES // 2 - labels)))
    bounds = jnp.concatenate([bounds, bounds], axis=1)
    key_places = [part.reshape(1, -1) for part in jnp.split(key_place, key_parts)]
    return query_place, key_places, limits, bounds


def labels_at(position, values, count):
    at = position[:, None, :] == jnp.arange(count, dtype=I32)[None, :, None]
    return jnp.sum(jnp.where(at, values[:, None, :], 0), axis=-1, dtype=I32)


def by_slots(normed, slots_of, route_index, codes, index, capacity, weight):
    wide_count = codes.shape[0]
    slots = wide_count * capacity
    packed, codes = lax.optimization_barrier((pack(slots_of, route_index, normed, slots * BLK), codes))
    arrived = exchange(packed, wide_count)
    mine = (codes // (2 * BLK)) == index
    rank = jnp.where(mine, earlier_sum(mine.astype(I32)), -1)
    found = labels_at(rank, codes % (2 * BLK) + 1, capacity).reshape(slots)
    live = found > 0
    label = jnp.where(live, (found - 1) // BLK, -1)
    fill = jnp.where(live, (found - 1) % BLK + 1, 0)
    places = sorted_places(label, fill, slots, 2, 1, min(TILE, slots * BLK))
    query = arrange(places, arrived, weight)
    mixture = rotated_attention(places, query, [arrived], weight, arrived.shape[0], 4)
    return [exchange(mixture, wide_count)]


def lower_mask(size):
    return jnp.where(iota((size, size), 0) < iota((size, size), 1), 1.0, 0.0).astype(BF16)


def ones_where(condition):
    return jnp.where(condition, 1.0, 0.0).astype(BF16)


def to_row(column):
    size = column.shape[0]
    same = iota((size, size), 0) == iota((size, size), 1)
    return jnp.sum(jnp.where(same, column, 0.0), axis=0, keepdims=True)


def route_kernel(
    wide_count, capacity, unit, here_ref, codes_ref, starts_ref, slots_ref, straddle_ref
):
    block_count = codes_ref.shape[1]
    lane = iota((1, LANES), 1)
    destination = codes_ref[...] // (2 * BLK)
    worst = jnp.zeros((1, LANES), F32)
    for side in range(2):
        part = destination[side * wide_count : (side + 1) * wide_count]
        held = jnp.zeros((wide_count, LANES), F32)
        for d in range(wide_count):
            count = jnp.sum(jnp.where(part == d, 1.0, 0.0), axis=1, keepdims=True)
            held = jnp.where(lane == d, count, held)
        load = jnp.sum(held, axis=0, keepdims=True)
        starts = jnp.zeros((wide_count, LANES), F32)
        for d in range(wide_count):
            other = load[:, d : d + 1]
            earlier = (other > load) | ((other == load) & (d < lane))
            starts = starts + jnp.where(earlier, held[:, d : d + 1], 0.0)
        starts_ref[pl.ds(side * wide_count, wide_count), :] = starts
        run = jnp.floor(starts * (1.0 / unit))
        last = jnp.floor((starts + held - 1.0) * (1.0 / unit))
        low = jnp.min(jnp.where(held > 0.0, run, 1e6), axis=0, keepdims=True)
        high = jnp.max(jnp.where(held > 0.0, last, -1.0), axis=0, keepdims=True)
        worst = jnp.maximum(worst, jnp.where((high > low) & (lane < wide_count), 1.0, 0.0))
    straddle_ref[0, 0] = jnp.max(worst).astype(I32)

    core = here_ref[0]
    index = core * wide_count + here_ref[1]
    own = codes_ref[pl.ds(index, 1), :] // (2 * BLK)
    start = starts_ref[pl.ds(index, 1), :]
    member = own == iota((wide_count, block_count), 0)
    rank = mm(ones_where(member), lower_mask(block_count))
    rank = jnp.sum(jnp.where(member, rank, 0.0), axis=0, keepdims=True)
    place = rank
    for d in range(wide_count):
        place = place + jnp.where(own == d, start[:, d : d + 1], 0.0)
    place = place.astype(I32)
    run, within = place // unit, place % unit
    half = unit // 2
    away = (within // half != core).astype(I32)
    slots_ref[0:1, :] = away * (block_count // 2) + run * half + within % half
    slots_ref[1:2, :] = own * capacity + rank.astype(I32)


def route(codes, here, wide_count, capacity, unit):
    devices, block_count = codes.shape
    full = lambda shape: pl.BlockSpec(shape, lambda _: (0, 0))
    return pl.pallas_call(
        functools.partial(route_kernel, wide_count, capacity, unit),
        grid=(1,),
        in_specs=[pl.BlockSpec(memory_space=pltpu.SMEM), whole(codes)],
        out_specs=[
            full((devices, LANES)), full((8, block_count)), pl.BlockSpec(memory_space=pltpu.SMEM),
        ],
        out_shape=[
            jax.ShapeDtypeStruct((devices, LANES), F32),
            jax.ShapeDtypeStruct((8, block_count), I32),
            jax.ShapeDtypeStruct((1, 1), I32),
        ],
        compiler_params=params(),
        name="route",
    )(here, codes)


def plan_kernel(
    unit, tile, here_ref, codes_ref, starts_ref,
    query_ref, limits_ref, bounds_ref, *key_refs
):
    wide_count, block_count = codes_ref.shape[0] // 2, codes_ref.shape[1]
    half = unit // 2
    blocks = wide_count * half
    core, side, base = here_ref[0], here_ref[1] % 2, here_ref[1] // 2 * unit
    mine = pl.ds(pl.multiple_of(side * wide_count, wide_count), wide_count)
    codes = codes_ref[mine, :]
    destination = codes // (2 * BLK)
    members = jnp.concatenate([ones_where(destination == d) for d in range(wide_count)], axis=0)
    rank = mm(members, lower_mask(block_count))
    starts = starts_ref[mine, :]
    position = jnp.zeros(codes.shape, F32)
    for d in range(wide_count):
        at = starts[:, d : d + 1] + rank[d * wide_count : (d + 1) * wide_count]
        position = position + jnp.where(destination == d, at, 0.0)
    position = position.astype(I32) - base
    values = codes.astype(F32) + 1.0

    def labels_of(which):
        columns = []
        for source in range(wide_count):
            at = iota((half, block_count), 0) + which * half == position[source : source + 1]
            found = jnp.where(at, values[source : source + 1], 0.0)
            columns.append(jnp.sum(found, axis=1, keepdims=True))
        found = to_row(jnp.concatenate(columns, axis=0)).astype(I32) + (BLK - 1)
        member = found // BLK - 1 == iota((LANES, blocks), 0) % (LANES // 2)
        return member, jnp.where(member, (found % BLK + 1).astype(F32), 0.0)

    earlier = lower_mask(blocks)
    below = iota((LANES, LANES), 1) < iota((LANES, LANES), 0) % (LANES // 2)

    def begin(total):
        return jnp.sum(jnp.where(below, to_row(total), 0.0), axis=1, keepdims=True)

    def place_of(member, at):
        once = member & (iota(member.shape, 0) < LANES // 2)
        return jnp.sum(jnp.where(once, at, 0.0), axis=0, keepdims=True).astype(I32)

    parts = [labels_of(which) for which in (core, 1 - core)]
    own = parts[0][0]
    own_ones = ones_where(own)
    own_total = jnp.sum(jnp.where(own, 1.0, 0.0), axis=1, keepdims=True)
    own_start = begin(own_total)
    query = place_of(own, own_start + mm(own_ones, earlier))
    query_ref[...] = query

    totals = [jnp.sum(fill, axis=1, keepdims=True) for _, fill in parts]
    total = sum(totals)
    padded = jnp.floor((total + (tile - 1)) * (1.0 / tile)) * tile
    once = iota((LANES, 1), 0) < LANES // 2
    room = jnp.sum(jnp.where(once, padded, 0.0), axis=0, keepdims=True) <= 2 * blocks * BLK
    key_start = begin(jnp.where(room, padded, total))
    key_end = key_start + total
    spread = ones_where(iota((blocks, blocks * BLK), 1) // BLK == iota((blocks, blocks * BLK), 0))
    point = iota((1, blocks * BLK), 1) % BLK
    begins = key_start
    for ref, (member, fill), part_total in zip(key_refs, parts, totals):
        at = place_of(member, begins + mm(fill.astype(BF16), earlier))
        count = place_of(member, fill)
        digits = jnp.concatenate([at // 32, at % 32, count] + [jnp.zeros_like(at)] * 5, axis=0)
        digits = mm(digits.astype(F32).astype(BF16), spread).astype(I32)
        ref[...] = jnp.where(point < digits[2:3], digits[:1] * 32 + digits[1:2] + point, -1)
        begins = begins + part_total

    rows = [to_row(c) for c in (own_start * BLK, (own_start + own_total) * BLK, key_start, key_end)]
    bounds_ref[...] = jnp.concatenate(rows + [jnp.zeros_like(rows[0])] * 4, axis=0).astype(I32)
    step = query_step(blocks * BLK)
    first = (iota((8, LANES), 0) * step).astype(F32)
    meets = (rows[0] < first + step) & (rows[1] > first) & (rows[1] > rows[0])
    low = jnp.min(jnp.where(meets, rows[2], 1e6), axis=1, keepdims=True).astype(I32)
    high = jnp.max(jnp.where(meets, rows[3], 0.0), axis=1, keepdims=True).astype(I32)
    low_tile = low // tile
    count = (high + tile - 1) // tile - low_tile
    live = jnp.max(rows[3], axis=1, keepdims=True).astype(I32)
    lane = iota((8, LANES), 1)
    limits = jnp.where(lane == 0, low_tile, jnp.where(lane == 1, count, 0))
    limits = jnp.where(lane == 2, blocks * BLK, jnp.where(lane == 3, live, limits))
    limits_ref[...] = jnp.where((lane < 2) & (high <= 0), 0, limits)


def plan(here, codes, starts, unit, tile):
    wide_count = codes.shape[0] // 2
    rows = wide_count * unit // 2 * BLK
    shapes = [(1, rows // BLK), (8, LANES), (8, LANES)] + [(1, rows)] * 2
    full = lambda shape: pl.BlockSpec(shape, lambda _: (0, 0))
    outs = pl.pallas_call(
        functools.partial(plan_kernel, unit, tile),
        grid=(1,),
        in_specs=[pl.BlockSpec(memory_space=pltpu.SMEM), whole(codes), whole(starts)],
        out_specs=[full(shape) for shape in shapes],
        out_shape=[jax.ShapeDtypeStruct(shape, I32) for shape in shapes],
        compiler_params=params(),
        cost_estimate=pl.CostEstimate(flops=1 << 33, bytes_accessed=1 << 22, transcendentals=0),
        name="plan",
    )(here, codes, starts)
    return outs[0], outs[3:], outs[1], outs[2]


def by_chips(normed, slots, here, codes, starts, weight):
    wide_count, block_count = codes.shape[0] // 2, codes.shape[1]
    unit = 2 * block_count // wide_count
    units = wide_count // 2
    rows_half = block_count * BLK // 2
    swap = lambda array: lax.ppermute(array, "narrow", [(0, 1), (1, 0)])
    is_first = lax.axis_index("narrow") == 0

    taken = swap(pack(slots, 0, normed, rows_half, rows_half))
    arrived = exchange(pack_beside(here, slots, normed, taken, units), wide_count)
    tile = min(TILE, 2 * rows_half)
    places = plan(here, codes, starts, unit, tile)
    arrived, places = lax.optimization_barrier((arrived, places))
    partner = swap(arrived)
    query = arrange(places, arrived, weight)
    key_rows = 4 * rows_half

    mixture = rotated_attention(places, query, [arrived, partner], weight, key_rows, 6)
    both = exchange(mixture, wide_count).reshape(units, 2, rows_half // units, -1)
    given = jnp.where(is_first, both[:, 1], both[:, 0]).reshape(rows_half, -1)
    return [both, swap(given)]


def on_device(
    points, counts, destination, rotated_ball, qkv_first, out_first, qkv_second, out_second
):
    balls, share, width = points.shape
    wide_count, narrow_count = lax.axis_size("wide"), lax.axis_size("narrow")
    block_count = destination.size
    capacity = max(2, 2 * block_count // wide_count)

    flat = (block_count,)
    dest_flat = destination.reshape(flat)
    code = (dest_flat * 2 + rotated_ball.reshape(flat)) * BLK + counts.reshape(flat) - 1
    power = not wide_count & (wide_count - 1)
    paired = narrow_count == 2 and power and wide_count > 1 and 2 * wide_count <= LANES // 2
    paired = paired and block_count % wide_count == 0 and capacity * wide_count == 2 * block_count
    paired = paired and TILE <= block_count * BLK <= 8 * TILE and block_count % TILE == 0

    codes = code.reshape(1, 1, block_count)
    if paired:
        cores = [(0, 1), (1, 0)]
        chips = [(i, i ^ 1) for i in range(wide_count)]
        both = [(i, i ^ 3) for i in range(2 * wide_count)]
        mine = (codes, lax.ppermute(codes, "narrow", cores))
        theirs = (
            lax.ppermute(codes, "wide", chips), lax.ppermute(codes, ("wide", "narrow"), both)
        )
        lower = lax.axis_index("narrow") == 0
        codes = side_by_side(
            side_by_side(*mine, lower, 0), side_by_side(*theirs, lower, 0),
            (lax.axis_index("wide") & 1) == 0, 1,
        )
    elif power:
        codes = double(codes, "wide", 1, 1)
    query, kv, pooled, bias = first_projection(points, counts, qkv_first)
    if narrow_count == 2:
        coarse = [pooled, lax.ppermute(pooled, "narrow", [(0, 1), (1, 0)])]
    else:
        coarse = [gather_shares(pooled, "narrow", 1)]
    results = ()
    step = 2
    if power and step < wide_count:
        codes = double(codes, "wide", step, 1)
        step *= 2
    for ball in range(balls):
        if power:
            while step < wide_count and (step < 8 << ball or ball == balls - 1):
                coarse, codes = lax.optimization_barrier((coarse, codes))
                codes = double(codes, "wide", step, 1)
                step *= 2
        results = first_attention(ball, query, kv, coarse, bias, points, out_first, results)
    if not power:
        codes = gather_shares(codes, "wide", 1)
    layer_one, normed = results
    normed = normed.reshape(balls * share, width)

    core = lax.axis_index("narrow")
    here = jnp.stack([core, lax.axis_index("wide")]).astype(I32)

    def slot_route(codes, slots, route_index):
        index = lax.axis_index("wide")
        returned = by_slots(normed, slots, route_index, codes, index, capacity, qkv_second)
        return finish(here, slots, route_index, layer_one, out_second, returned)

    if not paired:
        onehot = (jnp.arange(wide_count, dtype=I32)[:, None] == dest_flat[None, :]).astype(I32)
        rank = jnp.sum(earlier_sum(onehot) * onehot, axis=0, dtype=I32)
        return slot_route(codes[0], (dest_flat * capacity + rank).reshape(1, -1), 0)

    unit = 2 * block_count // wide_count
    codes = codes.reshape(2 * wide_count, block_count)
    starts, slots, straddle = route(codes, here, wide_count, capacity, unit)
    def chip_route():
        returned = by_chips(normed, slots, here, codes, starts, qkv_second)
        return finish(here, slots, 0, layer_one, out_second, returned)

    def own_labels():
        return codes.reshape(2, wide_count, block_count)[core]

    return lax.cond(
        straddle[0, 0] == 0, chip_route, lambda: slot_route(own_labels(), slots, 1)
    )


def solution(mesh):
    split = P("wide", "narrow")
    in_specs = (P("wide", "narrow", None), split, split, split, P(), P(), P(), P())
    out_specs = P("wide", "narrow", None)
    return jax.shard_map(
        on_device, mesh=mesh, in_specs=in_specs, out_specs=out_specs, check_vma=False
    )
```
